128 devices in a mesh: expert: 32 (over x, y, z_lo), dp: 4 (over z_hi, core).
Axes of the slice: x: 4, y: 4, z: 4 (z_hi: 2, z_lo: 2; z = z_hi * 2 + z_lo), core: 2. Of those that a mesh axis runs over, the one named last changes fastest.
Arguments:
- tokens: bfloat16 [8192, 5120], P('expert'), may hold values from -6 to 6
- out_grad: bfloat16 [8192, 5120], P('expert'), may hold values from -6 to 6
- assignments: int32 [8192, 6], P('expert'), may hold values from 0 to 159, all different within a row; in each aligned block of 256 rows (0 to 255, 256 to 511, ...) at most 12 rows name the same one
- w_gate: bfloat16 [32, 5120, 768], P('expert', None, 'dp'), may hold values from -0.078125 to 0.078125
- w_up: bfloat16 [32, 5120, 768], P('expert', None, 'dp'), may hold values from -0.078125 to 0.078125
- w_down: bfloat16 [32, 768, 5120], P('expert', 'dp'), may hold values from -0.21875 to 0.21875
Outputs:
- in_grad: bfloat16 [8192, 5120], P('expert', 'dp')
- grad_gate: bfloat16 [32, 5120, 768], P('expert', None, 'dp')
- grad_up: bfloat16 [32, 5120, 768], P('expert', None, 'dp')
- grad_down: bfloat16 [32, 768, 5120], P('expert', 'dp')
The draws below stay inside these ranges and needn't reach their ends.
Inputs may be any that keep to these rules, and one draw needn't show every extreme that they name: `assignments`: each token names 6 different experts; among the 256 rows of one device (aligned blocks) no expert is named by more than 12 tokens.
All inputs are finite; a program needn't handle non-finite values.
Results may differ from the reference program's by a relative error of at most 0.0054.
Values may be sent and summed in bfloat16 or wider, within the bound.
A program may use at most 128 MiB of HBM per device.

```python
import math
import jax
import jax.numpy as jnp
import numpy as np
from jax import lax

D = 5120
EXPERTS = 160
TOPK = 6
FF = 768
TOK_DEV = 256
CAP = 12
EXP_WIN = 32
TOKENS = 8192
N_EXPERT = 32


def block_scale(key, shape, pieces, low, top_value):
    factor_of = 1.0
    for dim, blocks in pieces:
        heights = jax.random.uniform(jax.random.fold_in(jax.random.fold_in(key, 6), dim), (blocks,), jnp.float32, low / len(pieces), top_value / len(pieces))
        factor_of = factor_of * jnp.repeat(jnp.exp(heights), shape[dim] // blocks).reshape((-1,) + (1,) * (len(shape) - 1 - dim))
    return factor_of


def deal_out(stream_key, own, number, rows, amount, top, most, slope):
    order = jax.random.permutation(stream_key, amount)
    packed, ordinary = load_shares(amount, rows * top, most, slope, True), load_shares(amount, rows * top, most, slope, False)
    places = jnp.arange(amount)

    def named(tallies, turn):
        used = int((tallies > 0).sum())
        fixed = max(1, used // 4)
        shifted = fixed + (places - fixed + turn * (used - fixed)) % max(1, amount - fixed)
        return jnp.zeros((amount,), jnp.int32).at[order[jnp.where(places < fixed, places, shifted)]].set(jnp.asarray(tallies, jnp.int32))

    tallies = jnp.where(number % 4 == 0, named(packed, number // 4), named(ordinary, number - number // 4 - 1))
    mixed = jax.random.permutation(jax.random.fold_in(own, 3), amount)
    giver, sink = mixed[0:amount // 2 * 2:2], mixed[1:amount // 2 * 2:2]
    room = jnp.minimum(tallies[giver] - 1, most - tallies[sink]) // 2
    room = jnp.where((giver == order[0]) | (sink == order[0]) | (tallies[sink] == 0), 0, jnp.maximum(room, 0))
    shifted = jax.random.randint(jax.random.fold_in(own, 4), (amount // 2,), 0, 1 << 20) % (room + 1)
    tallies = tallies.at[giver].add(-shifted).at[sink].add(shifted)
    items = jnp.searchsorted(jnp.cumsum(tallies), jnp.arange(rows * top), side="right").astype(jnp.int32)
    listing = items.reshape(top, rows).T
    listing = listing[jax.random.permutation(jax.random.fold_in(own, 1), rows)]
    turn = jax.random.randint(jax.random.fold_in(own, 2), (rows, 1), 0, top)
    return jnp.take_along_axis(listing, (jnp.arange(top)[None, :] + turn) % top, axis=1)


def load_shares(amount, total, most, skew, full):
    weights = [(1 << 20) // math.isqrt(grade ** skew) + 1 for grade in range(1, amount + 1)]
    largest = most if full else min(most, max(-(-total // amount), total * weights[0] // sum(weights)))
    least = 1 if total - largest >= amount - 1 else 0
    holding, spare = [largest] + [least] * (amount - 1), total - largest - least * (amount - 1)
    while spare > 0:
        movable = [i for i in range(1, amount) if holding[i] < largest] or [i for i in range(1, amount) if holding[i] < most]
        pool, left = sum([weights[i] for i in movable]), spare
        for i in movable:
            addition = min(most - holding[i], max(1, left * weights[i] // pool), spare)
            holding[i] = holding[i] + addition
            spare = spare - addition
    return np.array(holding)


def gaussian(key, dims, deviation, limit, split=(), kind=jnp.bfloat16):
    factor_of = block_scale(key, dims, split, -0.22, 0.18) if split else 1.0
    drawn = jax.random.normal(key, dims, jnp.float32) * deviation * factor_of
    return jnp.minimum(jnp.maximum(drawn, -limit), limit).astype(kind)


def setup_inputs(seed: int = 0) -> dict:
    key_of = jax.random.split(jax.random.key(seed), 7)
    tokens = gaussian(key_of[0], (TOKENS, D), 1.0, 6.0, ((0, 32),))
    out_grad = gaussian(key_of[1], (TOKENS, D), 1.0, 6.0, ((0, 32),))
    assignments_keys = jax.random.split(jax.random.fold_in(key_of[2], 1), TOKENS // TOK_DEV)
    assignments_turns = jax.random.permutation(jax.random.fold_in(key_of[2], 3), TOKENS // TOK_DEV)
    assignments = jax.vmap(lambda own, number: deal_out(jax.random.fold_in(key_of[2], 2), own, number, TOK_DEV, EXPERTS, TOPK, CAP, 1))(assignments_keys, assignments_turns).reshape((TOKENS, TOPK))
    w_gate = gaussian(key_of[3], (EXP_WIN, D, FF), D ** -0.5, 0.078125, ((0, 32), (2, 4)))
    w_up = gaussian(key_of[4], (EXP_WIN, D, FF), D ** -0.5, 0.078125, ((0, 32), (2, 4)))
    w_down = gaussian(key_of[5], (EXP_WIN, FF, D), FF ** -0.5, 0.21875, ((0, 32), (1, 4)))
    return {"tokens": tokens, "out_grad": out_grad, "assignments": assignments, "w_gate": w_gate, "w_up": w_up, "w_down": w_down}


def expert_back(rows_x, rows_g, gate_w, up_w, down_w):
    a_val = jnp.dot(rows_x, gate_w, preferred_element_type=jnp.float32)
    b_val = jnp.dot(rows_x, up_w, preferred_element_type=jnp.float32)
    s_val = jax.nn.sigmoid(a_val)
    silu_val = a_val * s_val
    hidden = (silu_val * b_val).astype(jnp.bfloat16)
    d_hidden = jnp.einsum("rd,fd->rf", rows_g, down_w, preferred_element_type=jnp.float32)
    d_gate = (d_hidden * b_val * s_val * (1.0 + a_val * (1.0 - s_val))).astype(jnp.bfloat16)
    d_up = (d_hidden * silu_val).astype(jnp.bfloat16)
    g_gate = jnp.einsum("rd,rf->df", rows_x, d_gate, preferred_element_type=jnp.float32)
    g_up = jnp.einsum("rd,rf->df", rows_x, d_up, preferred_element_type=jnp.float32)
    g_down = jnp.einsum("rf,rd->fd", hidden, rows_g, preferred_element_type=jnp.float32)
    terms = jnp.einsum("rf,df->rd", d_gate, gate_w, preferred_element_type=jnp.float32)
    terms = terms + jnp.einsum("rf,df->rd", d_up, up_w, preferred_element_type=jnp.float32)
    return g_gate, g_up, g_down, terms


def reference(tokens, out_grad, assignments, w_gate, w_up, w_down):
    count = N_EXPERT * CAP
    ident = jnp.arange(EXP_WIN, dtype=jnp.int32)

    def step(carry, items):
        expert_id, gate_w, up_w, down_w = items
        member = jnp.any(assignments == expert_id, axis=1)
        order = jnp.argsort(jnp.where(member, 0, 1).astype(jnp.int32), stable=True)[:count].astype(jnp.int32)
        active = member[order]
        rows_x = jnp.where(active[:, None], tokens[order], jnp.zeros((), jnp.bfloat16))
        rows_g = jnp.where(active[:, None], out_grad[order], jnp.zeros((), jnp.bfloat16))
        g_gate, g_up, g_down, terms = expert_back(rows_x, rows_g, gate_w, up_w, down_w)
        rounded = lax.optimization_barrier(terms.astype(jnp.bfloat16))
        picked = jnp.where(active[:, None], rounded.astype(jnp.float32), jnp.float32(0.0))
        carry = carry.at[order].add(picked)
        return carry, (g_gate.astype(jnp.bfloat16), g_up.astype(jnp.bfloat16), g_down.astype(jnp.bfloat16))

    start = jnp.zeros(tokens.shape, jnp.float32)
    total, grads = lax.scan(step, start, (ident, w_gate, w_up, w_down))
    return total.astype(jnp.bfloat16), grads[0], grads[1], grads[2]
```

```python
import functools

import jax
import jax.numpy as jnp
from jax import lax
from jax.experimental import pallas as pl
from jax.experimental.pallas import tpu as pltpu
from jax.sharding import PartitionSpec as P

MESH = pl.DeviceIdType.MESH
BF, F32 = jnp.bfloat16, jnp.float32

D, FL, CAP, TOK = 5120, 192, 12, 256
Q, E8 = D // 4, D // 8
CHUNKS = (
    ((1, 2), (3, 2), (2, 1), (2, 3)),
    ((2, 0), (0, 2), (0, 0), (2, 2)),
    ((1, 1), (3, 3), (1, 3), (3, 1)),
    ((1, 0), (3, 0), (0, 1), (0, 3)),
)
NC = len(CHUNKS)
G = 4
B = G * CAP
M = G * B
R = 2 * B


def mm(a, b):
    return lax.dot_general(a, b, (((1,), (0,)), ((), ())), preferred_element_type=F32)


def mm_nt(a, b):
    return lax.dot_general(a, b, (((1,), (1,)), ((), ())), preferred_element_type=F32)


def mm_tn(a, b):
    return lax.dot_general(a, b, (((0,), (0,)), ((), ())), preferred_element_type=F32)


def iota(shape, dim):
    return lax.broadcasted_iota(jnp.int32, shape, dim)


def kernel(
    tok_hbm, grad_hbm, assign_ref, wg_hbm, wu_hbm, wd_hbm,
    in_hbm, gg_hbm, gu_hbm, gd_hbm,
    src, wg, wu, wd, codes, smat, perm, wide,
    pk_n, pk_c, rn, rc_relay, rc, rows, own, ex_send, ex_recv,
    z_send, z_recv, ret_send, ret_recv, unp, da_s, db_s, h_s,
    o_gg, o_gu, o_gd, o_in,
    ld_sem, out_sem, self_sem,
    pn_s, pn_r, pc_s, pc_r, zf_s, zf_r, sn_s, sn_r, sc_s, sc_r,
    ex_s, ex_r, zr_s, zr_r, rt_s, rt_r,
):
    e_idx, d_idx = lax.axis_index("expert"), lax.axis_index("dp")
    x, y, zl = e_idx // 8, (e_idx // 2) % 4, e_idx % 2
    zh, c = d_idx // 2, d_idx % 2

    def column(dx, dy):
        return ((x + dx) % 4) * 4 + (y + dy) % 4

    def plane(dx, dy):
        return (column(dx, dy) * 2 + zl, d_idx)

    def z_side(w):
        return ((x * 4 + y) * 2 + (1 - zl), 2 * w + c)

    z_far = (e_idx, 2 * (1 - zh) + c)
    sibling = (e_idx, 2 * zh + (1 - c))

    def remote(a, b, s, r, dev):
        return pltpu.make_async_remote_copy(
            src_ref=a, dst_ref=b, send_sem=s, recv_sem=r, device_id=dev, device_id_type=MESH
        )

    @pl.when(c == 0)
    def _():
        pltpu.make_async_copy(tok_hbm, src, ld_sem.at[0]).start()

    @pl.when(c == 1)
    def _():
        pltpu.make_async_copy(grad_hbm, src, ld_sem.at[0]).start()

    loads = [
        pltpu.make_async_copy(wg_hbm.at[0], wg, ld_sem.at[1]),
        pltpu.make_async_copy(wu_hbm.at[0], wu, ld_sem.at[2]),
        pltpu.make_async_copy(wd_hbm.at[0], wd, ld_sem.at[3]),
    ]
    barrier = pltpu.get_barrier_semaphore()
    offsets = [o for ch in CHUNKS for o in ch]
    partners = [plane(*o) for o in offsets if o != (0, 0)]
    partners += [z_side(0), z_side(1), z_far, sibling]
    for dev in partners:
        pl.semaphore_signal(barrier, inc=1, device_id=dev, device_id_type=MESH)

    lane = iota((TOK, 128), 1)
    member = jnp.zeros((TOK, 128), F32)
    for k in range(assign_ref.shape[1]):
        member = member + jnp.where(assign_ref[:, k : k + 1] == lane, 1.0, 0.0)
    member = member.astype(BF)
    t0, t1 = iota((TOK, TOK), 0), iota((TOK, TOK), 1)
    upto = jnp.where(t0 <= t1, 1.0, 0.0).astype(BF)
    eye = jnp.where(t0 == t1, 1.0, 0.0).astype(BF)
    codes[...] = mm_tn(member, eye) * mm_tn(member, upto)
    row = iota((B, TOK), 0)
    grp, want = row // CAP, (row % CAP + 1).astype(F32)
    for k in range(NC):
        for kind in range(2):
            z_of = zl if kind == 0 else 1 - zl
            code = jnp.zeros((B, TOK), F32)
            for i, o in enumerate(CHUNKS[k]):
                line = codes[pl.ds(column(*o) * 2 + z_of, 1), :]
                code = jnp.where(grp == i, jnp.broadcast_to(line, (B, TOK)), code)
            smat[k, kind * B : (kind + 1) * B, :] = jnp.where(code == want, 1.0, 0.0).astype(BF)
    r0, r1 = iota((M, M), 0), iota((M, M), 1)
    swapped = ((r0 // CAP) % 4) * B + (r0 // B) * CAP + r0 % CAP
    perm[...] = jnp.where(swapped == r1, 1.0, 0.0).astype(BF)

    pl.semaphore_wait(barrier, len(partners))
    pltpu.make_async_copy(tok_hbm, src, ld_sem.at[0]).wait()
    for load in loads:
        load.start()

    def slot(k, i):
        return pl.ds(k * M + i * B, B)

    def chunk(k):
        return pl.ds(k * M, M)

    def send_n(k, i):
        return remote(pk_n.at[slot(k, i)], rn.at[c, slot(k, i)], pn_s.at[k * G + i], pn_r.at[k * G + i],
                      plane(*CHUNKS[k][i]))

    def send_c(k, i):
        return remote(pk_c.at[slot(k, i)], rc_relay.at[slot(k, i)], pc_s.at[k * G + i], pc_r.at[k * G + i],
                      plane(*CHUNKS[k][i]))

    def self_copies(k, i):
        return (
            pltpu.make_async_copy(pk_n.at[slot(k, i)], rn.at[c, slot(k, i)], self_sem.at[0]),
            pltpu.make_async_copy(pk_c.at[slot(k, i)], rc_relay.at[slot(k, i)], self_sem.at[1]),
        )

    def pack(k):
        for q in range(4):
            cols = pl.ds(q * Q, Q)
            wide[:, cols] = mm(smat[k], src[:, cols]).astype(BF)
        stack_n = jnp.concatenate([wide[0:B, q * Q : (q + 1) * Q] for q in range(4)], axis=0)
        pk_n[chunk(k), :] = mm(perm[...], stack_n).astype(BF)
        stack_c = jnp.concatenate(
            [wide[B:R, pl.ds(pl.multiple_of(zh * (D // 2) + j * E8, 128), E8)] for j in range(4)], axis=0
        )
        pk_c[chunk(k), :] = mm(perm[...], stack_c).astype(BF)
        for i, o in enumerate(CHUNKS[k]):
            if o == (0, 0):
                for cp in self_copies(k, i):
                    cp.start()
            else:
                send_n(k, i).start()
                send_c(k, i).start()

    def z_forward(k, w):
        return remote(rc_relay.at[chunk(k)], rc.at[c, zh, chunk(k)], zf_s.at[k * 2 + w], zf_r.at[k * 2 + zh],
                      z_side(w))

    def z_forward_in(k, w):
        return remote(rc_relay.at[chunk(k)], rc.at[c, w, chunk(k)], zf_s.at[k * 2 + w], zf_r.at[k * 2 + w],
                      z_side(w))

    def core_n(k, a):
        return remote(rn.at[a, chunk(k)], rn.at[a, chunk(k)], sn_s.at[k], sn_r.at[k], sibling)

    def core_c(k, a, w):
        return remote(rc.at[a, w, chunk(k)], rc.at[a, w, chunk(k)], sc_s.at[k * 2 + w], sc_r.at[k * 2 + w], sibling)

    def arrive(k):
        for i, o in enumerate(CHUNKS[k]):
            if o == (0, 0):
                for cp in self_copies(k, i):
                    cp.wait()
            else:
                send_n(k, i).wait_recv()
                send_c(k, i).wait_recv()
        for w in range(2):
            z_forward(k, w).start()
        core_n(k, c).start()

    def relay(k):
        for w in range(2):
            z_forward_in(k, w).wait_recv()
            core_c(k, c, w).start()

    def compute(k):
        core_n(k, 1 - c).wait_recv()
        for w in range(2):
            core_c(k, 1 - c, w).wait_recv()
        base = k * R
        for a in range(2):
            flat = mm(perm[...], rn[a, chunk(k), :]).astype(BF)
            for q in range(4):
                rows[a, base : base + B, q * Q : (q + 1) * Q] = flat[q * B : (q + 1) * B]
            for w in range(2):
                flat = mm(perm[...], rc[a, w, chunk(k), :]).astype(BF)
                for j in range(4):
                    at = w * (D // 2) + j * E8
                    rows[a, base + B : base + R, at : at + E8] = flat[j * B : (j + 1) * B]

        def forward(q, acc):
            cols = pl.ds(pl.multiple_of(q * Q, 128), Q)
            xt = rows[0, pl.ds(base, R), cols]
            gt = rows[1, pl.ds(base, R), cols]
            return (
                acc[0] + mm(xt, wg[cols, :]),
                acc[1] + mm(xt, wu[cols, :]),
                acc[2] + mm_nt(gt, wd[:, cols]),
            )

        zero = jnp.zeros((R, FL), F32)
        a_v, b_v, dh = lax.fori_loop(0, 4, forward, (zero, zero, zero))
        s_v = jax.nn.sigmoid(a_v)
        silu = a_v * s_v
        h_s[base : base + R, :] = (silu * b_v).astype(BF)
        da = (dh * b_v * s_v * (1.0 + a_v * (1.0 - s_v))).astype(BF)
        db = (dh * silu).astype(BF)
        da_s[base : base + R, :] = da
        db_s[base : base + R, :] = db

        def terms(w, core):
            at = pl.ds(pl.multiple_of((2 * w + core) * Q, 128), Q)
            return mm_nt(da, wg[at, :]) + mm_nt(db, wu[at, :])

        for w in range(2):
            ex_send[k, w] = terms(w, 1 - c).astype(BF)
        core_ex(k).start()
        for w in range(2):
            own[k % 2, w] = terms(w, c)

    def core_ex(k):
        return remote(ex_send.at[k], ex_recv.at[k], ex_s.at[k], ex_r.at[k], sibling)

    def z_far_copy(k):
        return remote(z_send.at[k, 0], z_recv.at[k, 0], zr_s.at[k * 3], zr_r.at[k * 3], z_far)

    def z_side_copy(k, w):
        return remote(z_send.at[k, 1 + w], z_recv.at[k, 1 + zh], zr_s.at[k * 3 + 1 + w], zr_r.at[k * 3 + 1 + zh],
                      z_side(w))

    def z_side_in(k, w):
        return remote(z_send.at[k, 1 + w], z_recv.at[k, 1 + w], zr_s.at[k * 3 + 1 + w], zr_r.at[k * 3 + 1 + w],
                      z_side(w))

    def z_reduce(k):
        core_ex(k).wait_recv()
        p = k % 2
        far = own[p, 1 - zh, 0:B, :] + ex_recv[k, 1 - zh, 0:B, :].astype(F32)
        z_send[k, 0] = far.astype(BF)
        z_far_copy(k).start()
        for w in range(2):
            z_send[k, 1 + w] = (own[p, w, B:R, :] + ex_recv[k, w, B:R, :].astype(F32)).astype(BF)
            z_side_copy(k, w).start()

    def back(k, i):
        dx, dy = CHUNKS[k][i]
        return remote(ret_send.at[slot(k, i)], ret_recv.at[slot(k, i)], rt_s.at[k * G + i], rt_r.at[k * G + i],
                      plane(-dx, -dy))

    def self_back(k, i):
        return pltpu.make_async_copy(ret_send.at[slot(k, i)], ret_recv.at[slot(k, i)], self_sem.at[2])

    def give_back(k):
        p = k % 2
        z_far_copy(k).wait_recv()
        mine = own[p, zh, 0:B, :] + ex_recv[k, zh, 0:B, :].astype(F32) + z_recv[k, 0].astype(F32)
        for w in range(2):
            z_side_in(k, w).wait_recv()
        side = z_recv[k, 1].astype(F32) + z_recv[k, 2].astype(F32)
        mine, side = mine.astype(BF), side.astype(BF)
        stack = jnp.concatenate([mine[:, :E8], side[:, :E8], mine[:, E8:], side[:, E8:]], axis=0)
        ret_send[chunk(k), :] = mm(perm[...], stack).astype(BF)
        for i, o in enumerate(CHUNKS[k]):
            if o == (0, 0):
                self_back(k, i).start()
            else:
                back(k, i).start()

    def collect(k):
        for i, o in enumerate(CHUNKS[k]):
            if o == (0, 0):
                self_back(k, i).wait()
            else:
                back(k, i).wait_recv()
        flat = mm(perm[...], ret_recv[chunk(k), :]).astype(BF)
        for hf in range(2):
            unp[k * R : (k + 1) * R, hf * E8 : (hf + 1) * E8] = flat[hf * R : (hf + 1) * R]

    outs = [
        pltpu.make_async_copy(o_gg, gg_hbm.at[0], out_sem.at[0]),
        pltpu.make_async_copy(o_gu, gu_hbm.at[0], out_sem.at[1]),
        pltpu.make_async_copy(o_gd, gd_hbm.at[0], out_sem.at[2]),
        pltpu.make_async_copy(o_in, in_hbm, out_sem.at[3]),
    ]

    def weight_grads():
        @pl.loop(0, 10)
        def _(t):
            cols = pl.ds(pl.multiple_of(t * 512, 128), 512)
            xt = rows[0, :, cols]
            o_gg[cols, :] = mm_tn(xt, da_s[...]).astype(BF)
            o_gu[cols, :] = mm_tn(xt, db_s[...]).astype(BF)
            o_gd[:, cols] = mm_tn(h_s[...], rows[1, :, cols]).astype(BF)

        for cp in outs[:3]:
            cp.start()

    for k in range(NC):
        pack(k)
    for load in loads:
        load.wait()
    for k in range(NC + 2):
        if k < NC:
            arrive(k)
        if 0 <= k - 1 < NC:
            relay(k - 1)
            compute(k - 1)
            z_reduce(k - 1)
        if k == NC:
            give_back(k - 2)
            weight_grads()
        elif 0 <= k - 2 < NC:
            give_back(k - 2)
    for k in range(NC):
        collect(k)
    smat_all = smat[...].reshape(NC * R, TOK)
    o_in[...] = mm_tn(smat_all, unp[...]).astype(BF)
    outs[3].start()

    for k in range(NC):
        for i, o in enumerate(CHUNKS[k]):
            if o != (0, 0):
                send_n(k, i).wait_send()
                send_c(k, i).wait_send()
                back(k, i).wait_send()
        for w in range(2):
            z_forward(k, w).wait_send()
            core_c(k, c, w).wait_send()
            z_side_copy(k, w).wait_send()
        core_n(k, c).wait_send()
        core_ex(k).wait_send()
        z_far_copy(k).wait_send()
    for cp in outs:
        cp.wait()


def per_device(tokens, out_grad, assignments, w_gate, w_up, w_down):
    hbm = pl.BlockSpec(memory_space=pl.ANY)
    vmem = pl.BlockSpec(memory_space=pltpu.VMEM)
    S = pltpu.SemaphoreType.DMA
    bf = lambda *shape: pltpu.VMEM(shape, BF)
    scratch = [
        bf(TOK, D), bf(D, FL), bf(D, FL), bf(FL, D),
        pltpu.VMEM((128, TOK), F32), bf(NC, R, TOK), bf(M, M), bf(R, D),
        bf(NC * M, Q), bf(NC * M, E8), bf(2, NC * M, Q), bf(NC * M, E8), bf(2, 2, NC * M, E8),
        bf(2, NC * R, D), pltpu.VMEM((2, 2, R, Q), F32), bf(NC, 2, R, Q), bf(NC, 2, R, Q),
        bf(NC, 3, B, Q), bf(NC, 3, B, Q), bf(NC * M, E8), bf(NC * M, E8), bf(NC * R, Q),
        bf(NC * R, FL), bf(NC * R, FL), bf(NC * R, FL),
        bf(D, FL), bf(D, FL), bf(FL, D), bf(TOK, Q),
        S((4,)), S((4,)), S((3,)),
        S((NC * G,)), S((NC * G,)), S((NC * G,)), S((NC * G,)),
        S((NC * 2,)), S((NC * 2,)), S((NC,)), S((NC,)), S((NC * 2,)), S((NC * 2,)),
        S((NC,)), S((NC,)), S((NC * 3,)), S((NC * 3,)), S((NC * G,)), S((NC * G,)),
    ]
    return tuple(pl.pallas_call(
        kernel,
        out_shape=(
            jax.ShapeDtypeStruct((TOK, Q), BF),
            jax.ShapeDtypeStruct((1, D, FL), BF),
            jax.ShapeDtypeStruct((1, D, FL), BF),
            jax.ShapeDtypeStruct((1, FL, D), BF),
        ),
        in_specs=[hbm, hbm, vmem, hbm, hbm, hbm],
        out_specs=(hbm, hbm, hbm, hbm),
        scratch_shapes=scratch,
        compiler_params=pltpu.CompilerParams(
            collective_id=0, has_side_effects=True, vmem_limit_bytes=62 * 2**20
        ),
        cost_estimate=pl.CostEstimate(flops=7 * 10**9, bytes_accessed=17 * 10**6, transcendentals=73728),
    )(tokens, out_grad, assignments, w_gate, w_up, w_down))


def solution(mesh):
    in_specs = (
        P("expert", None),
        P("expert", None),
        P("expert", None),
        P("expert", None, "dp"),
        P("expert", None, "dp"),
        P("expert", "dp", None),
    )
    out_specs = (
        P("expert", "dp"),
        P("expert", None, "dp"),
        P("expert", None, "dp"),
        P("expert", "dp", None),
    )
    return jax.shard_map(
        per_device, mesh=mesh, in_specs=in_specs, out_specs=out_specs, check_vma=False
    )
```

```python
import functools

import jax
import jax.numpy as jnp
from jax import lax
from jax.experimental import pallas as pl
from jax.experimental.pallas import tpu as pltpu
from jax.sharding import PartitionSpec as P

MESH = pl.DeviceIdType.MESH
BF, F32 = jnp.bfloat16, jnp.float32

D, FL, FP, CAP, TOK = 5120, 192, 256, 12, 256
Q, E8 = D // 4, D // 8
N_EXP = 32
CHUNKS = (
    ((1, 0), (3, 0), (0, 1), (0, 3)),
    ((1, 2), (3, 2), (2, 1), (2, 3)),
    ((1, 1), (3, 3), (1, 3), (3, 1)),
    ((2, 0), (0, 2), (0, 0), (2, 2)),
)
NC = len(CHUNKS)
G = 4
B = G * CAP
M = G * B
R = 2 * B
ALL = 2 * NC * B


def mm(a, b):
    return lax.dot_general(a, b, (((1,), (0,)), ((), ())), preferred_element_type=F32)


def mm_nt(a, b):
    return lax.dot_general(a, b, (((1,), (1,)), ((), ())), preferred_element_type=F32)


def mm_tn(a, b):
    return lax.dot_general(a, b, (((0,), (0,)), ((), ())), preferred_element_type=F32)


def iota(shape, dim):
    return lax.broadcasted_iota(jnp.int32, shape, dim)


def kernel(
    tok_hbm, grad_hbm, assign_ref, wg_hbm, wu_hbm, wd_hbm,
    o_in, o_gg, o_gu, o_gd,
    src, w_all, wt, codes, smat, perm, wide,
    pk_n, pk_c, rn, rc_relay, rc, rows, own, ex_send, ex_recv,
    zc_send, zc_recv, zn_send, zn_recv, ret_send, ret_recv, unp, dab_s, h_s, lhs,
    ld_sem, self_sem,
    pn_s, pn_r, pc_s, pc_r, zf_s, zf_r, sn_s, sn_r, sc_s, sc_r,
    ex_s, ex_r, zc_s, zc_r, zn_s, zn_r, rt_s, rt_r,
):
    e_idx, d_idx = lax.axis_index("expert"), lax.axis_index("dp")
    x, y, zl = e_idx // 8, (e_idx // 2) % 4, e_idx % 2
    zh, c = d_idx // 2, d_idx % 2

    def column(dx, dy):
        return ((x + dx) % 4) * 4 + (y + dy) % 4

    def plane(dx, dy):
        return (column(dx, dy) * 2 + zl, d_idx)

    def z_side(w):
        return ((x * 4 + y) * 2 + (1 - zl), 2 * w + c)

    z_far = (e_idx, 2 * (1 - zh) + c)
    sibling = (e_idx, 2 * zh + (1 - c))

    def remote(a, b, s, r, dev):
        return pltpu.make_async_remote_copy(
            src_ref=a, dst_ref=b, send_sem=s, recv_sem=r, device_id=dev, device_id_type=MESH
        )

    @pl.when(c == 0)
    def _():
        pltpu.make_async_copy(tok_hbm, src, ld_sem.at[0]).start()

    @pl.when(c == 1)
    def _():
        pltpu.make_async_copy(grad_hbm, src, ld_sem.at[0]).start()

    loads = [
        pltpu.make_async_copy(wg_hbm.at[0], w_all.at[pl.ds(0, FL)], ld_sem.at[1]),
        pltpu.make_async_copy(wu_hbm.at[0], w_all.at[pl.ds(FP, FL)], ld_sem.at[2]),
        pltpu.make_async_copy(wd_hbm.at[0], o_gd, ld_sem.at[3]),
    ]
    barrier = pltpu.get_barrier_semaphore()
    offsets = [o for ch in CHUNKS for o in ch]
    partners = [plane(*o) for o in offsets if o != (0, 0)]
    partners += [z_side(0), z_side(1), z_far, sibling]
    for dev in partners:
        pl.semaphore_signal(barrier, inc=1, device_id=dev, device_id_type=MESH)

    expert = iota((N_EXP, TOK), 0)
    member = jnp.zeros((N_EXP, TOK), F32)
    for k in range(assign_ref.shape[0]):
        member = member + jnp.where(assign_ref[k : k + 1, :] == expert, 1.0, 0.0)
    upto = jnp.where(iota((TOK, TOK), 0) <= iota((TOK, TOK), 1), 1.0, 0.0).astype(BF)
    codes[...] = member * mm(member.astype(BF), upto)
    row = iota((B, TOK), 0)
    grp, want = row // CAP, (row % CAP + 1).astype(F32)
    for kind in range(2):
        z_of = 1 - zl if kind == 0 else zl
        for k in range(NC):
            code = jnp.zeros((B, TOK), F32)
            for i, o in enumerate(CHUNKS[k]):
                line = codes[pl.ds(column(*o) * 2 + z_of, 1), :]
                code = jnp.where(grp == i, jnp.broadcast_to(line, (B, TOK)), code)
            at = (kind * NC + k) * B
            smat[at : at + B, :] = jnp.where(code == want, 1.0, 0.0).astype(BF)
    r0, r1 = iota((M, M), 0), iota((M, M), 1)
    swapped = ((r0 // CAP) % 4) * B + (r0 // B) * CAP + r0 % CAP
    perm[...] = jnp.where(swapped == r1, 1.0, 0.0).astype(BF)

    pl.semaphore_wait(barrier, len(partners))
    pltpu.make_async_copy(tok_hbm, src, ld_sem.at[0]).wait()
    for load in loads:
        load.start()
    for a in range(2):
        w_all[a * FP + FL : (a + 1) * FP, :] = jnp.zeros((FP - FL, D), BF)

    def slot(k, i):
        return pl.ds(k * M + i * B, B)

    def chunk(k):
        return pl.ds(k * M, M)

    def send_n(k, i):
        return remote(pk_n.at[slot(k, i)], rn.at[c, slot(k, i)], pn_s.at[k * G + i], pn_r.at[k * G + i],
                      plane(*CHUNKS[k][i]))

    def send_c(k, i):
        return remote(pk_c.at[slot(k, i)], rc_relay.at[slot(k, i)], pc_s.at[k * G + i], pc_r.at[k * G + i],
                      plane(*CHUNKS[k][i]))

    def self_n(k, i):
        return pltpu.make_async_copy(pk_n.at[slot(k, i)], rn.at[c, slot(k, i)], self_sem.at[0])

    def self_c(k, i):
        return pltpu.make_async_copy(pk_c.at[slot(k, i)], rc_relay.at[slot(k, i)], self_sem.at[1])

    def pack_c():
        for j in range(4):
            cols = pl.ds(pl.multiple_of(zh * (D // 2) + j * E8, 128), E8)
            wide[:, j * E8 : (j + 1) * E8] = mm(smat[0:M, :], src[:, cols]).astype(BF)
        for k in range(NC):
            stack = jnp.concatenate(
                [wide[k * B : (k + 1) * B, j * E8 : (j + 1) * E8] for j in range(4)], axis=0
            )
            pk_c[chunk(k), :] = mm(perm[...], stack).astype(BF)

    def pack_n():
        for q in range(4):
            wide[:, q * Q : (q + 1) * Q] = mm(smat[M : 2 * M, :], src[:, q * Q : (q + 1) * Q]).astype(BF)
        for k in range(NC):
            stack = jnp.concatenate([wide[k * B : (k + 1) * B, q * Q : (q + 1) * Q] for q in range(4)], axis=0)
            pk_n[chunk(k), :] = mm(perm[...], stack).astype(BF)

    def go(k, far, near):
        for i, o in enumerate(CHUNKS[k]):
            (near if o == (0, 0) else far)(k, i).start()

    def sent(k, far):
        for i, o in enumerate(CHUNKS[k]):
            if o != (0, 0):
                far(k, i).wait_send()

    def come(k, far, near):
        for i, o in enumerate(CHUNKS[k]):
            if o == (0, 0):
                near(k, i).wait()
            else:
                far(k, i).wait_recv()

    def go_c(k):
        go(k, send_c, self_c)

    def go_n(k):
        go(k, send_n, self_n)

    def sent_c(k):
        sent(k, send_c)

    def sent_n(k):
        sent(k, send_n)

    def z_forward(k, w):
        return remote(rc_relay.at[chunk(k)], rc.at[c, zh, chunk(k)], zf_s.at[k * 2 + w], zf_r.at[k * 2 + zh],
                      z_side(w))

    def z_forward_in(k, w):
        return remote(rc_relay.at[chunk(k)], rc.at[c, w, chunk(k)], zf_s.at[k * 2 + w], zf_r.at[k * 2 + w],
                      z_side(w))

    def core_n(k, a):
        return remote(rn.at[a, chunk(k)], rn.at[a, chunk(k)], sn_s.at[k], sn_r.at[k], sibling)

    def core_c(k, a, w):
        return remote(rc.at[a, w, chunk(k)], rc.at[a, w, chunk(k)], sc_s.at[k * 2 + w], sc_r.at[k * 2 + w], sibling)

    def arrive_c(k):
        come(k, send_c, self_c)
        for w in range(2):
            z_forward(k, w).start()

    def arrive_n(k):
        come(k, send_n, self_n)
        core_n(k, c).start()

    def relay(k):
        for w in range(2):
            z_forward_in(k, w).wait_recv()
            core_c(k, c, w).start()

    def unpack(kind, pair):
        base = (kind * 2 + pair) * R
        for half in range(2):
            k, at = pair * 2 + half, base + half * B
            if kind == 1:
                core_n(k, 1 - c).wait_recv()
                for a in range(2):
                    flat = mm(perm[...], rn[a, chunk(k), :]).astype(BF)
                    for q in range(4):
                        rows[a, at : at + B, q * Q : (q + 1) * Q] = flat[q * B : (q + 1) * B]
            else:
                for w in range(2):
                    core_c(k, 1 - c, w).wait_recv()
                for a in range(2):
                    for w in range(2):
                        flat = mm(perm[...], rc[a, w, chunk(k), :]).astype(BF)
                        for j in range(4):
                            col = w * (D // 2) + j * E8
                            rows[a, at : at + B, col : col + E8] = flat[j * B : (j + 1) * B]

    def hidden(kind, pair):
        base = (kind * 2 + pair) * R

        def forward(q, acc):
            cols = pl.ds(pl.multiple_of(q * Q, 128), Q)
            xt = rows[0, pl.ds(base, R), cols]
            gt = rows[1, pl.ds(base, R), cols]
            return (
                acc[0] + mm(xt, wt[cols, 0 : 2 * FP]),
                acc[1] + mm(gt, wt[cols, 2 * FP : 3 * FP]),
            )

        ab, dh = lax.fori_loop(0, 4, forward, (jnp.zeros((R, 2 * FP), F32), jnp.zeros((R, FP), F32)))
        a_v, b_v = ab[:, :FP], ab[:, FP:]
        s_v = jax.nn.sigmoid(a_v)
        silu = a_v * s_v
        h_s[base : base + R, :] = (silu * b_v).astype(BF)
        dab_s[base : base + R, :FP] = (dh * b_v * s_v * (1.0 + a_v * (1.0 - s_v))).astype(BF)
        dab_s[base : base + R, FP:] = (dh * silu).astype(BF)

    def terms(kind, pair):
        group = kind * 2 + pair
        base = group * R

        def term(w, core):
            at = pl.ds(pl.multiple_of((2 * w + core) * Q, 128), Q)
            return mm(dab_s[base : base + R, :], w_all[0 : 2 * FP, at])

        for w in range(2):
            ex_send[group, w] = term(w, 1 - c).astype(BF)
        core_ex(group).start()
        for w in range(2):
            own[pair, w] = term(w, c)

    def core_ex(group):
        return remote(ex_send.at[group], ex_recv.at[group], ex_s.at[group], ex_r.at[group], sibling)

    def z_far_copy(pair):
        return remote(zn_send.at[pair], zn_recv.at[pair], zn_s.at[pair], zn_r.at[pair], z_far)

    def z_side_copy(pair, w):
        return remote(zc_send.at[pair, w], zc_recv.at[pair, zh], zc_s.at[pair * 2 + w], zc_r.at[pair * 2 + zh],
                      z_side(w))

    def z_side_in(pair, w):
        return remote(zc_send.at[pair, w], zc_recv.at[pair, w], zc_s.at[pair * 2 + w], zc_r.at[pair * 2 + w],
                      z_side(w))

    def z_reduce(kind, pair):
        group = kind * 2 + pair
        core_ex(group).wait_recv()
        if kind == 1:
            zn_send[pair] = (own[pair, 1 - zh] + ex_recv[group, 1 - zh].astype(F32)).astype(BF)
            z_far_copy(pair).start()
        else:
            for w in range(2):
                zc_send[pair, w] = (own[pair, w] + ex_recv[group, w].astype(F32)).astype(BF)
                z_side_copy(pair, w).start()

    def z_come(pair):
        for w in range(2):
            z_side_in(pair, w).wait_recv()
        z_far_copy(pair).wait_recv()

    def back(k, i):
        dx, dy = CHUNKS[k][i]
        return remote(ret_send.at[slot(k, i)], ret_recv.at[slot(k, i)], rt_s.at[k * G + i], rt_r.at[k * G + i],
                      plane(-dx, -dy))

    def self_back(k, i):
        return pltpu.make_async_copy(ret_send.at[slot(k, i)], ret_recv.at[slot(k, i)], self_sem.at[2])

    def give_back(k):
        pair, at = k // 2, pl.ds((k % 2) * B, B)
        mine = own[pair, zh, at, :] + ex_recv[2 + pair, zh, at, :].astype(F32) + zn_recv[pair, at, :].astype(F32)
        side = zc_recv[pair, 0, at, :].astype(F32) + zc_recv[pair, 1, at, :].astype(F32)
        mine, side = mine.astype(BF), side.astype(BF)
        stack = jnp.concatenate([mine[:, :E8], side[:, :E8], mine[:, E8:], side[:, E8:]], axis=0)
        ret_send[chunk(k), :] = mm(perm[...], stack).astype(BF)
        go(k, back, self_back)

    def collect(k):
        come(k, back, self_back)
        flat = mm(perm[...], ret_recv[chunk(k), :]).astype(BF)
        for hf in range(2):
            for kind in range(2):
                at, of = (kind * NC + k) * B, (hf * 2 + 1 - kind) * B
                unp[at : at + B, hf * E8 : (hf + 1) * E8] = flat[of : of + B]

    def turn_weights(part):
        loads[part].wait()
        tail = jnp.zeros((FP - FL, 512), BF)

        @pl.loop(0, 10)
        def _(t):
            cols = pl.ds(pl.multiple_of(t * 512, 128), 512)
            mine = o_gd[:, cols] if part == 2 else w_all[part * FP : part * FP + FL, cols]
            full = jnp.concatenate([mine, tail], axis=0)
            wt[cols, part * FP : (part + 1) * FP] = full.T

    def turn_rows():
        lhs[0 : 2 * FP, :] = dab_s[...].astype(F32).T.astype(BF)
        lhs[2 * FP : 3 * FP, :] = h_s[...].astype(F32).T.astype(BF)
        lhs[3 * FP :, :] = smat[...].astype(F32).T.astype(BF)

    def wgrads(first, last):
        @pl.loop(first, last)
        def _(t):
            cols = pl.ds(pl.multiple_of(t * 512, 128), 512)
            both = mm(lhs[0 : 2 * FP, :], rows[0, :, cols])
            o_gg[:, cols] = both[0:FL].astype(BF)
            o_gu[:, cols] = both[FP : FP + FL].astype(BF)
            o_gd[:, cols] = mm(lhs[2 * FP : 3 * FP, :], rows[1, :, cols])[0:FL].astype(BF)

    pack_c()
    go_c(0)
    pack_n()
    sent_c(0)
    go_c(1)
    arrive_c(0)
    turn_weights(0)
    turn_weights(1)
    sent_c(1)
    go_c(2)
    go_c(3)
    arrive_c(1)
    turn_weights(2)
    sent_c(2)
    sent_c(3)
    go_n(0)
    go_n(1)
    arrive_c(2)
    arrive_c(3)
    relay(0)
    relay(1)
    go_n(2)
    go_n(3)
    unpack(0, 0)
    hidden(0, 0)
    terms(0, 0)
    relay(2)
    z_reduce(0, 0)
    relay(3)
    arrive_n(0)
    arrive_n(1)
    unpack(0, 1)
    hidden(0, 1)
    terms(0, 1)
    unpack(1, 0)
    z_reduce(0, 1)
    hidden(1, 0)
    terms(1, 0)
    arrive_n(2)
    arrive_n(3)
    z_reduce(1, 0)
    unpack(1, 1)
    hidden(1, 1)
    terms(1, 1)
    z_reduce(1, 1)
    z_come(0)
    give_back(0)
    give_back(1)
    turn_rows()
    wgrads(0, 5)
    z_come(1)
    give_back(2)
    give_back(3)
    wgrads(5, 10)
    for k in range(NC):
        collect(k)
    o_in[...] = mm(lhs[3 * FP :, :], unp[...]).astype(BF)

    for k in range(NC):
        sent_n(k)
    for k in range(NC):
        sent(k, back)
        for w in range(2):
            z_forward(k, w).wait_send()
            core_c(k, c, w).wait_send()
        core_n(k, c).wait_send()
        core_ex(k).wait_send()
    for pair in range(2):
        for w in range(2):
            z_side_copy(pair, w).wait_send()
        z_far_copy(pair).wait_send()


def hand_over(n, *refs):
    src, dst, sem = refs[:n], refs[n : 2 * n], refs[2 * n]
    outs = [
        pltpu.make_async_copy(src[i], dst[i] if i == 0 else dst[i].at[0], sem.at[i]) for i in range(n)
    ]
    for cp in outs:
        cp.start()
    for cp in outs:
        cp.wait()


def per_device(tokens, out_grad, assignments, w_gate, w_up, w_down):
    hbm = pl.BlockSpec(memory_space=pl.ANY)
    vmem = pl.BlockSpec(memory_space=pltpu.VMEM)
    S = pltpu.SemaphoreType.DMA
    bf = lambda *shape: pltpu.VMEM(shape, BF)
    scratch = [
        bf(TOK, D), bf(2 * FP, D), bf(D, 3 * FP),
        pltpu.VMEM((N_EXP, TOK), F32), bf(ALL, TOK), bf(M, M), bf(M, D),
        bf(NC * M, Q), bf(NC * M, E8), bf(2, NC * M, Q), bf(NC * M, E8), bf(2, 2, NC * M, E8),
        bf(2, ALL, D), pltpu.VMEM((2, 2, R, Q), F32), bf(NC, 2, R, Q), bf(NC, 2, R, Q),
        bf(2, 2, R, Q), bf(2, 2, R, Q), bf(2, R, Q), bf(2, R, Q), bf(NC * M, E8), bf(NC * M, E8), bf(ALL, Q),
        bf(ALL, 2 * FP), bf(ALL, FP), bf(4 * FP, ALL),
        S((4,)), S((3,)),
        S((NC * G,)), S((NC * G,)), S((NC * G,)), S((NC * G,)),
        S((NC * 2,)), S((NC * 2,)), S((NC,)), S((NC,)), S((NC * 2,)), S((NC * 2,)),
        S((NC,)), S((NC,)), S((4,)), S((4,)), S((2,)), S((2,)), S((NC * G,)), S((NC * G,)),
    ]
    made = lambda *shape: jax.ShapeDtypeStruct(shape, BF)
    made_here = pl.pallas_call(
        kernel,
        out_shape=(bf(TOK, Q), bf(FL, D), bf(FL, D), bf(FL, D)),
        in_specs=[hbm, hbm, vmem, hbm, hbm, hbm],
        out_specs=(vmem,) * 4,
        scratch_shapes=scratch,
        compiler_params=pltpu.CompilerParams(
            collective_id=0, has_side_effects=True, vmem_limit_bytes=56 * 2**20
        ),
        cost_estimate=pl.CostEstimate(flops=8 * 10**9, bytes_accessed=15 * 10**6, transcendentals=73728),
    )(tokens, out_grad, assignments.T, w_gate.swapaxes(1, 2), w_up.swapaxes(1, 2), w_down)
    in_grad, g_gate, g_up, g_down = pl.pallas_call(
        functools.partial(hand_over, 4),
        out_shape=(made(TOK, Q), made(1, FL, D), made(1, FL, D), made(1, FL, D)),
        in_specs=[vmem] * 4,
        out_specs=(hbm,) * 4,
        scratch_shapes=[S((4,))],
        compiler_params=pltpu.CompilerParams(vmem_limit_bytes=2 * 2**20),
                cost_estimate=pl.CostEstimate(flops=0, bytes_accessed=7 * 10**6, transcendentals=0),
    )(*[pltpu.with_memory_space_constraint(a, pltpu.VMEM) for a in made_here])
    return in_grad, g_gate.swapaxes(1, 2), g_up.swapaxes(1, 2), g_down


def solution(mesh):
    in_specs = (
        P("expert", None),
        P("expert", None),
        P("expert", None),
        P("expert", None, "dp"),
        P("expert", None, "dp"),
        P("expert", "dp", None),
    )
    out_specs = (
        P("expert", "dp"),
        P("expert", None, "dp"),
        P("expert", None, "dp"),
        P("expert", "dp", None),
    )
    return jax.shard_map(
        per_device, mesh=mesh, in_specs=in_specs, out_specs=out_specs, check_vma=False
    )
```

```python
import functools

import jax
import jax.numpy as jnp
from jax import lax
from jax.experimental import pallas as pl
from jax.experimental.pallas import tpu as pltpu
from jax.sharding import PartitionSpec as P

MESH = pl.DeviceIdType.MESH
BF, F32 = jnp.bfloat16, jnp.float32

D, FL, FP, CAP, TOK = 5120, 192, 256, 12, 256
Q, E8 = D // 4, D // 8
N_EXP = 32
PARTS = 4
CHUNKS = (
    ((1, 1), (3, 3), (1, 3), (3, 1)),
    ((2, 0), (0, 2), (0, 0), (2, 2)),
    ((1, 2), (3, 2), (2, 1), (2, 3)),
    ((1, 0), (3, 0), (0, 1), (0, 3)),
)
NC = len(CHUNKS)
G = 4
B = G * CAP
M = G * B
R = 2 * B
EX = ((0, R, 0), (R, R, 1), (2 * R, R, 2), (3 * R, B, 3), (3 * R + B, B, 4))
ALL = 2 * NC * B


def mm(a, b):
    return lax.dot_general(a, b, (((1,), (0,)), ((), ())), preferred_element_type=F32)


def mm_nt(a, b):
    return lax.dot_general(a, b, (((1,), (1,)), ((), ())), preferred_element_type=F32)


def mm_tn(a, b):
    return lax.dot_general(a, b, (((0,), (0,)), ((), ())), preferred_element_type=F32)


def iota(shape, dim):
    return lax.broadcasted_iota(jnp.int32, shape, dim)


def kernel(
    tok_hbm, grad_hbm, assign_ref, wg_hbm, wu_hbm, wd_hbm,
    o_in, o_gg, o_gu, o_gd,
    src, w_all, wt, codes, smat, perm, wide,
    pk_n, pk_c, rn, rc_relay, rc, rows, own, ex_send, ex_recv,
    zc_send, zc_recv, zn_send, zn_recv, ret_send, ret_recv, unp, dab_s, h_s, lhs,
    ld_sem, self_sem,
    pn_s, pn_r, pc_s, pc_r, zf_s, zf_r, sn_s, sn_r, sc_s, sc_r,
    ex_s, ex_r, zc_s, zc_r, zn_s, zn_r, rt_s, rt_r,
):
    e_idx, d_idx = lax.axis_index("expert"), lax.axis_index("dp")
    x, y, zl = e_idx // 8, (e_idx // 2) % 4, e_idx % 2
    zh, c = d_idx // 2, d_idx % 2

    def column(dx, dy):
        return ((x + dx) % 4) * 4 + (y + dy) % 4

    def plane(dx, dy):
        return (column(dx, dy) * 2 + zl, d_idx)

    def z_side(w):
        return ((x * 4 + y) * 2 + (1 - zl), 2 * w + c)

    z_far = (e_idx, 2 * (1 - zh) + c)
    sibling = (e_idx, 2 * zh + (1 - c))

    def remote(a, b, s, r, dev):
        return pltpu.make_async_remote_copy(
            src_ref=a, dst_ref=b, send_sem=s, recv_sem=r, device_id=dev, device_id_type=MESH
        )

    @pl.when(c == 0)
    def _():
        pltpu.make_async_copy(tok_hbm, src, ld_sem.at[0]).start()

    @pl.when(c == 1)
    def _():
        pltpu.make_async_copy(grad_hbm, src, ld_sem.at[0]).start()

    loads = [
        pltpu.make_async_copy(wg_hbm.at[0], w_all.at[pl.ds(0, FL)], ld_sem.at[1]),
        pltpu.make_async_copy(wu_hbm.at[0], w_all.at[pl.ds(FP, FL)], ld_sem.at[2]),
        pltpu.make_async_copy(wd_hbm.at[0], o_gd, ld_sem.at[3]),
    ]
    barrier = pltpu.get_barrier_semaphore()
    offsets = [o for ch in CHUNKS for o in ch]
    partners = [plane(*o) for o in offsets if o != (0, 0)]
    partners += [z_side(0), z_side(1), z_far, sibling]
    for dev in partners:
        pl.semaphore_signal(barrier, inc=1, device_id=dev, device_id_type=MESH)

    expert = iota((N_EXP, TOK), 0)
    member = jnp.zeros((N_EXP, TOK), F32)
    for k in range(assign_ref.shape[0]):
        member = member + jnp.where(assign_ref[k : k + 1, :] == expert, 1.0, 0.0)
    upto = jnp.where(iota((TOK, TOK), 0) <= iota((TOK, TOK), 1), 1.0, 0.0).astype(BF)
    codes[...] = member * mm(member.astype(BF), upto)
    row = iota((B, TOK), 0)
    grp, want = row // CAP, (row % CAP + 1).astype(F32)

    def choose(kind, k):
        z_of = 1 - zl if kind == 0 else zl
        code = jnp.zeros((B, TOK), F32)
        for i, o in enumerate(CHUNKS[k]):
            line = codes[pl.ds(column(*o) * 2 + z_of, 1), :]
            code = jnp.where(grp == i, jnp.broadcast_to(line, (B, TOK)), code)
        at = (kind * NC + k) * B
        smat[at : at + B, :] = jnp.where(code == want, 1.0, 0.0).astype(BF)

    choose(0, 0)
    r0, r1 = iota((M, M), 0), iota((M, M), 1)
    swapped = ((r0 // CAP) % 4) * B + (r0 // B) * CAP + r0 % CAP
    perm[...] = jnp.where(swapped == r1, 1.0, 0.0).astype(BF)

    pl.semaphore_wait(barrier, len(partners))
    pltpu.make_async_copy(tok_hbm, src, ld_sem.at[0]).wait()
    for load in loads:
        load.start()
    for a in range(2):
        w_all[a * FP + FL : (a + 1) * FP, :] = jnp.zeros((FP - FL, D), BF)

    def slot(k, i):
        return pl.ds(k * M + i * B, B)

    def chunk(k):
        return pl.ds(k * M, M)

    def send_n(k, i):
        return remote(pk_n.at[slot(k, i)], rn.at[c, slot(k, i)], pn_s.at[k * G + i], pn_r.at[k * G + i],
                      plane(*CHUNKS[k][i]))

    def send_c(k, i):
        return remote(pk_c.at[slot(k, i)], rc_relay.at[slot(k, i)], pc_s.at[k * G + i], pc_r.at[k * G + i],
                      plane(*CHUNKS[k][i]))

    def self_n(k, i):
        return pltpu.make_async_copy(pk_n.at[slot(k, i)], rn.at[c, slot(k, i)], self_sem.at[0])

    def self_c(k, i):
        return pltpu.make_async_copy(pk_c.at[slot(k, i)], rc_relay.at[slot(k, i)], self_sem.at[1])

    def pack_c(k):
        at = slice(k * B, (k + 1) * B)
        for j in range(4):
            cols = pl.ds(pl.multiple_of(zh * (D // 2) + j * E8, 128), E8)
            wide[at, j * E8 : (j + 1) * E8] = mm(smat[at, :], src[:, cols]).astype(BF)
        stack = jnp.concatenate([wide[at, j * E8 : (j + 1) * E8] for j in range(4)], axis=0)
        pk_c[chunk(k), :] = mm(perm[...], stack).astype(BF)

    def pack_n():
        for q in range(4):
            wide[:, q * Q : (q + 1) * Q] = mm(smat[M : 2 * M, :], src[:, q * Q : (q + 1) * Q]).astype(BF)
        for k in range(NC):
            stack = jnp.concatenate([wide[k * B : (k + 1) * B, q * Q : (q + 1) * Q] for q in range(4)], axis=0)
            pk_n[chunk(k), :] = mm(perm[...], stack).astype(BF)

    def go(k, far, near):
        for i, o in enumerate(CHUNKS[k]):
            (near if o == (0, 0) else far)(k, i).start()

    def sent(k, far):
        for i, o in enumerate(CHUNKS[k]):
            if o != (0, 0):
                far(k, i).wait_send()

    def come(k, far, near):
        for i, o in enumerate(CHUNKS[k]):
            if o == (0, 0):
                near(k, i).wait()
            else:
                far(k, i).wait_recv()

    def go_c(k):
        go(k, send_c, self_c)

    def go_n(k):
        go(k, send_n, self_n)

    def sent_c(k):
        sent(k, send_c)

    def sent_n(k):
        sent(k, send_n)

    def z_forward(k, w):
        return remote(rc_relay.at[chunk(k)], rc.at[c, zh, chunk(k)], zf_s.at[k * 2 + w], zf_r.at[k * 2 + zh],
                      z_side(w))

    def z_forward_in(k, w):
        return remote(rc_relay.at[chunk(k)], rc.at[c, w, chunk(k)], zf_s.at[k * 2 + w], zf_r.at[k * 2 + w],
                      z_side(w))

    def core_n(k, a):
        return remote(rn.at[a, chunk(k)], rn.at[a, chunk(k)], sn_s.at[k], sn_r.at[k], sibling)

    def core_c(k, a, w):
        return remote(rc.at[a, w, chunk(k)], rc.at[a, w, chunk(k)], sc_s.at[k * 2 + w], sc_r.at[k * 2 + w], sibling)

    def arrive_c(k):
        come(k, send_c, self_c)
        for w in range(2):
            z_forward(k, w).start()

    def arrive_n(k):
        come(k, send_n, self_n)
        core_n(k, c).start()

    def relay(k):
        for w in range(2):
            z_forward_in(k, w).wait_recv()
            core_c(k, c, w).start()

    def unpack(kind, pair, halves=(0, 1)):
        base = (kind * 2 + pair) * R
        for half in halves:
            k, at = pair * 2 + half, base + half * B
            if kind == 1:
                core_n(k, 1 - c).wait_recv()
                for a in range(2):
                    flat = mm(perm[...], rn[a, chunk(k), :]).astype(BF)
                    for q in range(4):
                        rows[a, at : at + B, q * Q : (q + 1) * Q] = flat[q * B : (q + 1) * B]
            else:
                for w in range(2):
                    core_c(k, 1 - c, w).wait_recv()
                for a in range(2):
                    for w in range(2):
                        flat = mm(perm[...], rc[a, w, chunk(k), :]).astype(BF)
                        for j in range(4):
                            col = w * (D // 2) + j * E8
                            rows[a, at : at + B, col : col + E8] = flat[j * B : (j + 1) * B]

    def hidden(base, m):

        def forward(q, acc):
            cols = pl.ds(pl.multiple_of(q * Q, 128), Q)
            xt = rows[0, pl.ds(base, m), cols]
            gt = rows[1, pl.ds(base, m), cols]
            return (
                acc[0] + mm(xt, wt[cols, 0 : 2 * FP]),
                acc[1] + mm(gt, wt[cols, 2 * FP : 3 * FP]),
            )

        ab, dh = lax.fori_loop(0, 4, forward, (jnp.zeros((m, 2 * FP), F32), jnp.zeros((m, FP), F32)))
        a_v, b_v = ab[:, :FP], ab[:, FP:]
        s_v = jax.nn.sigmoid(a_v)
        silu = a_v * s_v
        h_s[base : base + m, :] = (silu * b_v).astype(BF)
        dab_s[base : base + m, :FP] = (dh * b_v * s_v * (1.0 + a_v * (1.0 - s_v))).astype(BF)
        dab_s[base : base + m, FP:] = (dh * silu).astype(BF)

    def terms(base, m, part):
        group, lo = base // R, base % R
        at_rows = slice(lo, lo + m)

        def term(w, core):
            at = pl.ds(pl.multiple_of((2 * w + core) * Q, 128), Q)
            return mm(dab_s[base : base + m, :], w_all[0 : 2 * FP, at])

        for w in range(2):
            ex_send[group, w, at_rows] = term(w, 1 - c).astype(BF)
        core_ex(base, m, part).start()
        for w in range(2):
            own[group % 2, w, at_rows] = term(w, c)

    def core_ex(base, m, part):
        group, at = base // R, pl.ds(base % R, m)
        return remote(ex_send.at[group, :, at], ex_recv.at[group, :, at], ex_s.at[part], ex_r.at[part], sibling)

    def z_far_copy(k):
        return remote(zn_send.at[k], zn_recv.at[k], zn_s.at[k], zn_r.at[k], z_far)

    def go_far(k):
        z_far_copy(k).start()

    def z_side_copy(pair, w):
        return remote(zc_send.at[pair, w], zc_recv.at[pair, zh], zc_s.at[pair * 2 + w], zc_r.at[pair * 2 + zh],
                      z_side(w))

    def z_side_in(pair, w):
        return remote(zc_send.at[pair, w], zc_recv.at[pair, w], zc_s.at[pair * 2 + w], zc_r.at[pair * 2 + w],
                      z_side(w))

    def come_ex(part):
        core_ex(*EX[part]).wait_recv()

    def reduce_side(pair):
        group = pair
        core_ex(group * R, R, group).wait_recv()
        for w in range(2):
            zc_send[pair, w] = (own[pair, w] + ex_recv[group, w].astype(F32)).astype(BF)
            z_side_copy(pair, w).start()

    def reduce_far(k):
        pair, at = k // 2, pl.ds((k % 2) * B, B)
        far = own[pair, 1 - zh, at, :] + ex_recv[2 + pair, 1 - zh, at, :].astype(F32)
        zn_send[k] = far.astype(BF)

    def back(k, i):
        dx, dy = CHUNKS[k][i]
        return remote(ret_send.at[slot(k, i)], ret_recv.at[slot(k, i)], rt_s.at[k * G + i], rt_r.at[k * G + i],
                      plane(-dx, -dy))

    def self_back(k, i):
        return pltpu.make_async_copy(ret_send.at[slot(k, i)], ret_recv.at[slot(k, i)], self_sem.at[2])

    def give_back(k):
        pair, at = k // 2, pl.ds((k % 2) * B, B)
        if k % 2 == 0:
            for w in range(2):
                z_side_in(pair, w).wait_recv()
        z_far_copy(k).wait_recv()
        mine = own[pair, zh, at, :] + ex_recv[2 + pair, zh, at, :].astype(F32) + zn_recv[k].astype(F32)
        side = zc_recv[pair, 0, at, :].astype(F32) + zc_recv[pair, 1, at, :].astype(F32)
        mine, side = mine.astype(BF), side.astype(BF)
        stack = jnp.concatenate([mine[:, :E8], side[:, :E8], mine[:, E8:], side[:, E8:]], axis=0)
        ret_send[chunk(k), :] = mm(perm[...], stack).astype(BF)
        go(k, back, self_back)

    def collect(k):
        come(k, back, self_back)
        flat = mm(perm[...], ret_recv[chunk(k), :]).astype(BF)
        for hf in range(2):
            for kind in range(2):
                at, of = (kind * NC + k) * B, (hf * 2 + 1 - kind) * B
                unp[at : at + B, hf * E8 : (hf + 1) * E8] = flat[of : of + B]

    def turn_weights(part):
        loads[part].wait()
        tail = jnp.zeros((FP - FL, 512), BF)

        @pl.loop(0, 10)
        def _(t):
            cols = pl.ds(pl.multiple_of(t * 512, 128), 512)
            mine = o_gd[:, cols] if part == 2 else w_all[part * FP : part * FP + FL, cols]
            full = jnp.concatenate([mine, tail], axis=0)
            wt[cols, part * FP : (part + 1) * FP] = full.T

    def total():
        o_in[...] = mm(lhs[3 * FL :, :], unp[...]).astype(BF)

    def turn_rows():
        for a in range(2):
            lhs[a * FL : (a + 1) * FL, :] = dab_s[:, a * FP : (a + 1) * FP].astype(F32).T[0:FL].astype(BF)
        lhs[2 * FL : 3 * FL, :] = h_s[...].astype(F32).T[0:FL].astype(BF)
        lhs[3 * FL :, :] = smat[...].astype(F32).T.astype(BF)

    def wgrads(first, last):
        @pl.loop(first, last)
        def _(t):
            cols = pl.ds(pl.multiple_of(t * 512, 128), 512)
            both = mm(lhs[0 : 2 * FL, :], rows[0, :, cols])
            o_gg[:, cols] = both[0:FL].astype(BF)
            o_gu[:, cols] = both[FL : 2 * FL].astype(BF)
            o_gd[:, cols] = mm(lhs[2 * FL : 3 * FL, :], rows[1, :, cols]).astype(BF)

    pack_c(0)
    go_c(0)
    for k in range(1, NC):
        choose(0, k)
        pack_c(k)
    sent_c(0)
    go_c(1)
    for k in range(NC):
        choose(1, k)
    pack_n()
    arrive_c(0)
    sent_c(1)
    go_c(2)
    go_c(3)
    turn_weights(0)
    arrive_c(1)
    go_n(0)
    turn_weights(1)
    turn_weights(2)
    relay(0)
    sent_c(2)
    sent_c(3)
    go_n(1)
    relay(1)
    arrive_c(2)
    arrive_c(3)
    unpack(0, 0)
    hidden(*EX[0][:2])
    terms(*EX[0])
    reduce_side(0)
    arrive_n(0)
    arrive_n(1)
    go_n(2)
    relay(2)
    unpack(1, 0)
    hidden(*EX[2][:2])
    go_n(3)
    relay(3)
    terms(*EX[2])
    unpack(0, 1)
    come_ex(2)
    reduce_far(0)
    go_far(0)
    reduce_far(1)
    hidden(*EX[1][:2])
    go_far(1)
    terms(*EX[1])
    arrive_n(2)
    unpack(1, 1, (0,))
    reduce_side(1)
    hidden(*EX[3][:2])
    arrive_n(3)
    terms(*EX[3])
    give_back(0)
    come_ex(3)
    reduce_far(2)
    go_far(2)
    unpack(1, 1, (1,))
    give_back(1)
    hidden(*EX[4][:2])
    terms(*EX[4])
    turn_rows()
    come_ex(4)
    reduce_far(3)
    go_far(3)
    give_back(2)
    wgrads(0, 5)
    give_back(3)
    wgrads(5, 10)
    for k in range(NC):
        collect(k)
    total()
    def drain():
        for k in range(NC):
            sent_n(k)
        for k in range(NC):
            sent(k, back)
            for w in range(2):
                z_forward(k, w).wait_send()
                core_c(k, c, w).wait_send()
            core_n(k, c).wait_send()
        for pair in range(2):
            for w in range(2):
                z_side_copy(pair, w).wait_send()
        for k in range(NC):
            z_far_copy(k).wait_send()
        for ex in EX:
            core_ex(*ex).wait_send()

    drain()


def hand_over(n, *refs):
    src, dst, sem = refs[:n], refs[n : 2 * n], refs[2 * n]
    outs = []
    for i in range(n):
        to = dst[i] if i == 0 else dst[i].at[0]
        part = src[i].shape[0] // PARTS
        for p in range(PARTS):
            at = pl.ds(p * part, part)
            outs.append(pltpu.make_async_copy(src[i].at[at], to.at[at], sem.at[i * PARTS + p]))
    for cp in outs:
        cp.start()
    for cp in outs:
        cp.wait()


def per_device(tokens, out_grad, assignments, w_gate, w_up, w_down):
    hbm = pl.BlockSpec(memory_space=pl.ANY)
    vmem = pl.BlockSpec(memory_space=pltpu.VMEM)
    S = pltpu.SemaphoreType.DMA
    bf = lambda *shape: pltpu.VMEM(shape, BF)
    scratch = [
        bf(TOK, D), bf(2 * FP, D), bf(D, 3 * FP),
        pltpu.VMEM((N_EXP, TOK), F32), bf(ALL, TOK), bf(M, M), bf(M, D),
        bf(NC * M, Q), bf(NC * M, E8), bf(2, NC * M, Q), bf(NC * M, E8), bf(2, 2, NC * M, E8),
        bf(2, ALL, D), pltpu.VMEM((2, 2, R, Q), F32), bf(NC, 2, R, Q), bf(NC, 2, R, Q),
        bf(2, 2, R, Q), bf(2, 2, R, Q), bf(NC, B, Q), bf(NC, B, Q), bf(NC * M, E8), bf(NC * M, E8), bf(ALL, Q),
        bf(ALL, 2 * FP), bf(ALL, FP), bf(3 * FL + TOK, ALL),
        S((4,)), S((3,)),
        S((NC * G,)), S((NC * G,)), S((NC * G,)), S((NC * G,)),
        S((NC * 2,)), S((NC * 2,)), S((NC,)), S((NC,)), S((NC * 2,)), S((NC * 2,)),
        S((len(EX),)), S((len(EX),)), S((4,)), S((4,)), S((NC,)), S((NC,)), S((NC * G,)), S((NC * G,)),
    ]
    made = lambda *shape: jax.ShapeDtypeStruct(shape, BF)
    made_here = pl.pallas_call(
        kernel,
        out_shape=(bf(TOK, Q), bf(FL, D), bf(FL, D), bf(FL, D)),
        in_specs=[hbm, hbm, vmem, hbm, hbm, hbm],
        out_specs=(vmem,) * 4,
        scratch_shapes=scratch,
        compiler_params=pltpu.CompilerParams(
            collective_id=0, has_side_effects=True, vmem_limit_bytes=56 * 2**20
        ),
        cost_estimate=pl.CostEstimate(flops=8 * 10**9, bytes_accessed=15 * 10**6, transcendentals=73728),
    )(tokens, out_grad, assignments.T, w_gate.swapaxes(1, 2), w_up.swapaxes(1, 2), w_down)
    in_grad, g_gate, g_up, g_down = pl.pallas_call(
        functools.partial(hand_over, 4),
        out_shape=(made(TOK, Q), made(1, FL, D), made(1, FL, D), made(1, FL, D)),
        in_specs=[vmem] * 4,
        out_specs=(hbm,) * 4,
        scratch_shapes=[S((4 * PARTS,))],
        compiler_params=pltpu.CompilerParams(vmem_limit_bytes=2 * 2**20),
                cost_estimate=pl.CostEstimate(flops=0, bytes_accessed=7 * 10**6, transcendentals=0),
    )(*[pltpu.with_memory_space_constraint(a, pltpu.VMEM) for a in made_here])
    return in_grad, g_gate.swapaxes(1, 2), g_up.swapaxes(1, 2), g_down


def solution(mesh):
    in_specs = (
        P("expert", None),
        P("expert", None),
        P("expert", None),
        P("expert", None, "dp"),
        P("expert", None, "dp"),
        P("expert", "dp", None),
    )
    out_specs = (
        P("expert", "dp"),
        P("expert", None, "dp"),
        P("expert", None, "dp"),
        P("expert", "dp", None),
    )
    return jax.shard_map(
        per_device, mesh=mesh, in_specs=in_specs, out_specs=out_specs, check_vma=False
    )
```

```python
import functools

import jax
import jax.numpy as jnp
from jax import lax
from jax.experimental import pallas as pl
from jax.experimental.pallas import tpu as pltpu
from jax.sharding import PartitionSpec as P

MESH = pl.DeviceIdType.MESH
BF, F32 = jnp.bfloat16, jnp.float32

D, FL, FP, CAP, TOK = 5120, 192, 256, 12, 256
Q, E8 = D // 4, D // 8
N_EXP = 32
PARTS = 4
CHUNKS = (
    ((1, 0), (3, 0), (0, 1), (0, 3)),
    ((1, 2), (3, 2), (2, 1), (2, 3)),
    ((1, 1), (3, 3), (1, 3), (3, 1)),
    ((2, 0), (0, 2), (0, 0), (2, 2)),
)
NC = len(CHUNKS)
G = 4
B = G * CAP
M = G * B
R = 2 * B
EX = ((0, R, 0), (R, R, 1), (2 * R, R, 2), (3 * R, B, 3), (3 * R + B, B, 4))
ALL = 2 * NC * B


def mm(a, b):
    return lax.dot_general(a, b, (((1,), (0,)), ((), ())), preferred_element_type=F32)


def mm_nt(a, b):
    return lax.dot_general(a, b, (((1,), (1,)), ((), ())), preferred_element_type=F32)


def mm_tn(a, b):
    return lax.dot_general(a, b, (((0,), (0,)), ((), ())), preferred_element_type=F32)


def iota(shape, dim):
    return lax.broadcasted_iota(jnp.int32, shape, dim)


def kernel(
    tok_hbm, grad_hbm, assign_ref, wg_hbm, wu_hbm, wd_hbm,
    o_in, o_gg, o_gu, o_gd,
    src, w_all, wt, codes, smat, perm, wide,
    pk_n, pk_c, rn, rc_relay, rc, rows, own, ex_send, ex_recv,
    zc_send, zc_recv, zn_send, zn_recv, ret_send, ret_recv, unp, dab_s, h_s, lhs,
    ld_sem, self_sem,
    pn_s, pn_r, pc_s, pc_r, zf_s, zf_r, sn_s, sn_r, sc_s, sc_r,
    ex_s, ex_r, zc_s, zc_r, zn_s, zn_r, rt_s, rt_r,
):
    e_idx, d_idx = lax.axis_index("expert"), lax.axis_index("dp")
    x, y, zl = e_idx // 8, (e_idx // 2) % 4, e_idx % 2
    zh, c = d_idx // 2, d_idx % 2

    def column(dx, dy):
        return ((x + dx) % 4) * 4 + (y + dy) % 4

    def plane(dx, dy):
        return (column(dx, dy) * 2 + zl, d_idx)

    def z_side(w):
        return ((x * 4 + y) * 2 + (1 - zl), 2 * w + c)

    z_far = (e_idx, 2 * (1 - zh) + c)
    sibling = (e_idx, 2 * zh + (1 - c))

    def remote(a, b, s, r, dev):
        return pltpu.make_async_remote_copy(
            src_ref=a, dst_ref=b, send_sem=s, recv_sem=r, device_id=dev, device_id_type=MESH
        )

    @pl.when(c == 0)
    def _():
        pltpu.make_async_copy(tok_hbm, src, ld_sem.at[0]).start()

    @pl.when(c == 1)
    def _():
        pltpu.make_async_copy(grad_hbm, src, ld_sem.at[0]).start()

    loads = [
        pltpu.make_async_copy(wg_hbm.at[0], w_all.at[pl.ds(0, FL)], ld_sem.at[1]),
        pltpu.make_async_copy(wu_hbm.at[0], w_all.at[pl.ds(FP, FL)], ld_sem.at[2]),
        pltpu.make_async_copy(wd_hbm.at[0], o_gd, ld_sem.at[3]),
    ]
    barrier = pltpu.get_barrier_semaphore()
    offsets = [o for ch in CHUNKS for o in ch]
    partners = [plane(*o) for o in offsets if o != (0, 0)]
    partners += [z_side(0), z_side(1), z_far, sibling]
    for dev in partners:
        pl.semaphore_signal(barrier, inc=1, device_id=dev, device_id_type=MESH)

    expert = iota((N_EXP, TOK), 0)
    member = jnp.zeros((N_EXP, TOK), F32)
    for k in range(assign_ref.shape[0]):
        member = member + jnp.where(assign_ref[k : k + 1, :] == expert, 1.0, 0.0)
    upto = jnp.where(iota((TOK, TOK), 0) <= iota((TOK, TOK), 1), 1.0, 0.0).astype(BF)
    codes[...] = member * mm(member.astype(BF), upto)
    row = iota((B, TOK), 0)
    grp, want = row // CAP, (row % CAP + 1).astype(F32)

    def choose(kind, k):
        z_of = 1 - zl if kind == 0 else zl
        code = jnp.zeros((B, TOK), F32)
        for i, o in enumerate(CHUNKS[k]):
            line = codes[pl.ds(column(*o) * 2 + z_of, 1), :]
            code = jnp.where(grp == i, jnp.broadcast_to(line, (B, TOK)), code)
        at = (kind * NC + k) * B
        smat[at : at + B, :] = jnp.where(code == want, 1.0, 0.0).astype(BF)

    choose(0, 0)
    r0, r1 = iota((M, M), 0), iota((M, M), 1)
    swapped = ((r0 // CAP) % 4) * B + (r0 // B) * CAP + r0 % CAP
    perm[...] = jnp.where(swapped == r1, 1.0, 0.0).astype(BF)

    pl.semaphore_wait(barrier, len(partners))
    pltpu.make_async_copy(tok_hbm, src, ld_sem.at[0]).wait()
    for load in loads:
        load.start()
    for a in range(2):
        w_all[a * FP + FL : (a + 1) * FP, :] = jnp.zeros((FP - FL, D), BF)

    def slot(k, i):
        return pl.ds(k * M + i * B, B)

    def chunk(k):
        return pl.ds(k * M, M)

    def send_n(k, i):
        return remote(pk_n.at[slot(k, i)], rn.at[c, slot(k, i)], pn_s.at[k * G + i], pn_r.at[k * G + i],
                      plane(*CHUNKS[k][i]))

    def send_c(k, i):
        return remote(pk_c.at[slot(k, i)], rc_relay.at[slot(k, i)], pc_s.at[k * G + i], pc_r.at[k * G + i],
                      plane(*CHUNKS[k][i]))

    def self_n(k, i):
        return pltpu.make_async_copy(pk_n.at[slot(k, i)], rn.at[c, slot(k, i)], self_sem.at[0])

    def self_c(k, i):
        return pltpu.make_async_copy(pk_c.at[slot(k, i)], rc_relay.at[slot(k, i)], self_sem.at[1])

    def pack_c(k):
        at = slice(k * B, (k + 1) * B)
        for j in range(4):
            cols = pl.ds(pl.multiple_of(zh * (D // 2) + j * E8, 128), E8)
            wide[at, j * E8 : (j + 1) * E8] = mm(smat[at, :], src[:, cols]).astype(BF)
        stack = jnp.concatenate([wide[at, j * E8 : (j + 1) * E8] for j in range(4)], axis=0)
        pk_c[chunk(k), :] = mm(perm[...], stack).astype(BF)

    def pack_n():
        for q in range(4):
            wide[:, q * Q : (q + 1) * Q] = mm(smat[M : 2 * M, :], src[:, q * Q : (q + 1) * Q]).astype(BF)
        for k in range(NC):
            stack = jnp.concatenate([wide[k * B : (k + 1) * B, q * Q : (q + 1) * Q] for q in range(4)], axis=0)
            pk_n[chunk(k), :] = mm(perm[...], stack).astype(BF)

    def go(k, far, near):
        for i, o in enumerate(CHUNKS[k]):
            (near if o == (0, 0) else far)(k, i).start()

    def sent(k, far):
        for i, o in enumerate(CHUNKS[k]):
            if o != (0, 0):
                far(k, i).wait_send()

    def come(k, far, near):
        for i, o in enumerate(CHUNKS[k]):
            if o == (0, 0):
                near(k, i).wait()
            else:
                far(k, i).wait_recv()

    def go_c(k):
        go(k, send_c, self_c)

    def go_n(k):
        go(k, send_n, self_n)

    def sent_c(k):
        sent(k, send_c)

    def sent_n(k):
        sent(k, send_n)

    def z_forward(k, w):
        return remote(rc_relay.at[chunk(k)], rc.at[c, zh, chunk(k)], zf_s.at[k * 2 + w], zf_r.at[k * 2 + zh],
                      z_side(w))

    def z_forward_in(k, w):
        return remote(rc_relay.at[chunk(k)], rc.at[c, w, chunk(k)], zf_s.at[k * 2 + w], zf_r.at[k * 2 + w],
                      z_side(w))

    def core_n(k, a):
        return remote(rn.at[a, chunk(k)], rn.at[a, chunk(k)], sn_s.at[k], sn_r.at[k], sibling)

    def core_c(k, a, w):
        return remote(rc.at[a, w, chunk(k)], rc.at[a, w, chunk(k)], sc_s.at[k * 2 + w], sc_r.at[k * 2 + w], sibling)

    def arrive_c(k):
        come(k, send_c, self_c)
        for w in range(2):
            z_forward(k, w).start()

    def arrive_n(k):
        come(k, send_n, self_n)
        core_n(k, c).start()

    def relay(k):
        for w in range(2):
            z_forward_in(k, w).wait_recv()
            core_c(k, c, w).start()

    def unpack(kind, pair, halves=(0, 1)):
        base = (kind * 2 + pair) * R
        for half in halves:
            k, at = pair * 2 + half, base + half * B
            if kind == 1:
                core_n(k, 1 - c).wait_recv()
                for a in range(2):
                    flat = mm(perm[...], rn[a, chunk(k), :]).astype(BF)
                    for q in range(4):
                        rows[a, at : at + B, q * Q : (q + 1) * Q] = flat[q * B : (q + 1) * B]
            else:
                for w in range(2):
                    core_c(k, 1 - c, w).wait_recv()
                for a in range(2):
                    for w in range(2):
                        flat = mm(perm[...], rc[a, w, chunk(k), :]).astype(BF)
                        for j in range(4):
                            col = w * (D // 2) + j * E8
                            rows[a, at : at + B, col : col + E8] = flat[j * B : (j + 1) * B]

    def hidden(base, m):

        def forward(q, acc):
            cols = pl.ds(pl.multiple_of(q * Q, 128), Q)
            xt = rows[0, pl.ds(base, m), cols]
            gt = rows[1, pl.ds(base, m), cols]
            return (
                acc[0] + mm(xt, wt[cols, 0 : 2 * FP]),
                acc[1] + mm(gt, wt[cols, 2 * FP : 3 * FP]),
            )

        ab, dh = lax.fori_loop(0, 4, forward, (jnp.zeros((m, 2 * FP), F32), jnp.zeros((m, FP), F32)))
        a_v, b_v = ab[:, :FP], ab[:, FP:]
        s_v = jax.nn.sigmoid(a_v)
        silu = a_v * s_v
        h_s[base : base + m, :] = (silu * b_v).astype(BF)
        dab_s[base : base + m, :FP] = (dh * b_v * s_v * (1.0 + a_v * (1.0 - s_v))).astype(BF)
        dab_s[base : base + m, FP:] = (dh * silu).astype(BF)

    def terms(base, m, part):
        group, lo = base // R, base % R
        at_rows = slice(lo, lo + m)

        def term(w, core):
            at = pl.ds(pl.multiple_of((2 * w + core) * Q, 128), Q)
            return mm(dab_s[base : base + m, :], w_all[0 : 2 * FP, at])

        for w in range(2):
            ex_send[group, w, at_rows] = term(w, 1 - c).astype(BF)
        core_ex(base, m, part).start()
        for w in range(2):
            own[group % 2, w, at_rows] = term(w, c)

    def core_ex(base, m, part):
        group, at = base // R, pl.ds(base % R, m)
        return remote(ex_send.at[group, :, at], ex_recv.at[group, :, at], ex_s.at[part], ex_r.at[part], sibling)

    def z_far_copy(k):
        return remote(zn_send.at[k], zn_recv.at[k], zn_s.at[k], zn_r.at[k], z_far)

    def go_far(k):
        z_far_copy(k).start()

    def z_side_copy(pair, w):
        return remote(zc_send.at[pair, w], zc_recv.at[pair, zh], zc_s.at[pair * 2 + w], zc_r.at[pair * 2 + zh],
                      z_side(w))

    def z_side_in(pair, w):
        return remote(zc_send.at[pair, w], zc_recv.at[pair, w], zc_s.at[pair * 2 + w], zc_r.at[pair * 2 + w],
                      z_side(w))

    def come_ex(part):
        core_ex(*EX[part]).wait_recv()

    def reduce_side(pair):
        group = pair
        core_ex(group * R, R, group).wait_recv()
        for w in range(2):
            zc_send[pair, w] = (own[pair, w] + ex_recv[group, w].astype(F32)).astype(BF)
            z_side_copy(pair, w).start()

    def reduce_far(k):
        pair, at = k // 2, pl.ds((k % 2) * B, B)
        far = own[pair, 1 - zh, at, :] + ex_recv[2 + pair, 1 - zh, at, :].astype(F32)
        zn_send[k] = far.astype(BF)

    def back(k, i):
        dx, dy = CHUNKS[k][i]
        return remote(ret_send.at[slot(k, i)], ret_recv.at[slot(k, i)], rt_s.at[k * G + i], rt_r.at[k * G + i],
                      plane(-dx, -dy))

    def self_back(k, i):
        return pltpu.make_async_copy(ret_send.at[slot(k, i)], ret_recv.at[slot(k, i)], self_sem.at[2])

    def give_back(k):
        pair, at = k // 2, pl.ds((k % 2) * B, B)
        if k % 2 == 0:
            for w in range(2):
                z_side_in(pair, w).wait_recv()
        z_far_copy(k).wait_recv()
        mine = own[pair, zh, at, :] + ex_recv[2 + pair, zh, at, :].astype(F32) + zn_recv[k].astype(F32)
        side = zc_recv[pair, 0, at, :].astype(F32) + zc_recv[pair, 1, at, :].astype(F32)
        mine, side = mine.astype(BF), side.astype(BF)
        stack = jnp.concatenate([mine[:, :E8], side[:, :E8], mine[:, E8:], side[:, E8:]], axis=0)
        ret_send[chunk(k), :] = mm(perm[...], stack).astype(BF)
        go(k, back, self_back)

    def collect(k):
        come(k, back, self_back)
        flat = mm(perm[...], ret_recv[chunk(k), :]).astype(BF)
        for hf in range(2):
            for kind in range(2):
                at, of = (kind * NC + k) * B, (hf * 2 + 1 - kind) * B
                unp[at : at + B, hf * E8 : (hf + 1) * E8] = flat[of : of + B]

    def turn_weights(part):
        loads[part].wait()
        tail = jnp.zeros((FP - FL, 512), BF)

        @pl.loop(0, 10)
        def _(t):
            cols = pl.ds(pl.multiple_of(t * 512, 128), 512)
            mine = o_gd[:, cols] if part == 2 else w_all[part * FP : part * FP + FL, cols]
            full = jnp.concatenate([mine, tail], axis=0)
            wt[cols, part * FP : (part + 1) * FP] = full.T

    def total():
        o_in[...] = mm(lhs[3 * FL :, :], unp[...]).astype(BF)

    def turn_rows():
        for a in range(2):
            lhs[a * FL : (a + 1) * FL, :] = dab_s[:, a * FP : (a + 1) * FP].astype(F32).T[0:FL].astype(BF)
        lhs[2 * FL : 3 * FL, :] = h_s[...].astype(F32).T[0:FL].astype(BF)
        lhs[3 * FL :, :] = smat[...].astype(F32).T.astype(BF)

    def wgrads(first, last):
        @pl.loop(first, last)
        def _(t):
            cols = pl.ds(pl.multiple_of(t * 512, 128), 512)
            both = mm(lhs[0 : 2 * FL, :], rows[0, :, cols])
            o_gg[:, cols] = both[0:FL].astype(BF)
            o_gu[:, cols] = both[FL : 2 * FL].astype(BF)
            o_gd[:, cols] = mm(lhs[2 * FL : 3 * FL, :], rows[1, :, cols]).astype(BF)

    pack_c(0)
    go_c(0)
    for k in range(1, NC):
        choose(0, k)
        pack_c(k)
    sent_c(0)
    go_c(1)
    for k in range(NC):
        choose(1, k)
    pack_n()
    arrive_c(0)
    sent_c(1)
    go_c(2)
    go_c(3)
    turn_weights(0)
    arrive_c(1)
    go_n(0)
    turn_weights(1)
    turn_weights(2)
    relay(0)
    sent_c(2)
    sent_c(3)
    go_n(1)
    relay(1)
    arrive_c(2)
    arrive_c(3)
    unpack(0, 0)
    hidden(*EX[0][:2])
    terms(*EX[0])
    reduce_side(0)
    arrive_n(0)
    arrive_n(1)
    go_n(2)
    relay(2)
    unpack(1, 0)
    hidden(*EX[2][:2])
    go_n(3)
    relay(3)
    terms(*EX[2])
    unpack(0, 1)
    come_ex(2)
    reduce_far(0)
    go_far(0)
    reduce_far(1)
    hidden(*EX[1][:2])
    go_far(1)
    arrive_n(2)
    terms(*EX[1])
    unpack(1, 1, (0,))
    reduce_side(1)
    hidden(*EX[3][:2])
    arrive_n(3)
    terms(*EX[3])
    give_back(0)
    unpack(1, 1, (1,))
    come_ex(3)
    reduce_far(2)
    go_far(2)
    give_back(1)
    hidden(*EX[4][:2])
    terms(*EX[4])
    turn_rows()
    come_ex(4)
    reduce_far(3)
    go_far(3)
    give_back(2)
    wgrads(0, 5)
    give_back(3)
    wgrads(5, 10)
    for k in range(NC):
        collect(k)
    total()
    def drain():
        for k in range(NC):
            sent_n(k)
        for k in range(NC):
            sent(k, back)
            for w in range(2):
                z_forward(k, w).wait_send()
                core_c(k, c, w).wait_send()
            core_n(k, c).wait_send()
        for pair in range(2):
            for w in range(2):
                z_side_copy(pair, w).wait_send()
        for k in range(NC):
            z_far_copy(k).wait_send()
        for ex in EX:
            core_ex(*ex).wait_send()

    drain()


def hand_over(n, *refs):
    src, dst, sem = refs[:n], refs[n : 2 * n], refs[2 * n]
    outs = []
    for i in range(n):
        to = dst[i] if i == 0 else dst[i].at[0]
        part = src[i].shape[0] // PARTS
        for p in range(PARTS):
            at = pl.ds(p * part, part)
            outs.append(pltpu.make_async_copy(src[i].at[at], to.at[at], sem.at[i * PARTS + p]))
    for cp in outs:
        cp.start()
    for cp in outs:
        cp.wait()


def per_device(tokens, out_grad, assignments, w_gate, w_up, w_down):
    hbm = pl.BlockSpec(memory_space=pl.ANY)
    vmem = pl.BlockSpec(memory_space=pltpu.VMEM)
    S = pltpu.SemaphoreType.DMA
    bf = lambda *shape: pltpu.VMEM(shape, BF)
    scratch = [
        bf(TOK, D), bf(2 * FP, D), bf(D, 3 * FP),
        pltpu.VMEM((N_EXP, TOK), F32), bf(ALL, TOK), bf(M, M), bf(M, D),
        bf(NC * M, Q), bf(NC * M, E8), bf(2, NC * M, Q), bf(NC * M, E8), bf(2, 2, NC * M, E8),
        bf(2, ALL, D), pltpu.VMEM((2, 2, R, Q), F32), bf(NC, 2, R, Q), bf(NC, 2, R, Q),
        bf(2, 2, R, Q), bf(2, 2, R, Q), bf(NC, B, Q), bf(NC, B, Q), bf(NC * M, E8), bf(NC * M, E8), bf(ALL, Q),
        bf(ALL, 2 * FP), bf(ALL, FP), bf(3 * FL + TOK, ALL),
        S((4,)), S((3,)),
        S((NC * G,)), S((NC * G,)), S((NC * G,)), S((NC * G,)),
        S((NC * 2,)), S((NC * 2,)), S((NC,)), S((NC,)), S((NC * 2,)), S((NC * 2,)),
        S((len(EX),)), S((len(EX),)), S((4,)), S((4,)), S((NC,)), S((NC,)), S((NC * G,)), S((NC * G,)),
    ]
    made = lambda *shape: jax.ShapeDtypeStruct(shape, BF)
    made_here = pl.pallas_call(
        kernel,
        out_shape=(bf(TOK, Q), bf(FL, D), bf(FL, D), bf(FL, D)),
        in_specs=[hbm, hbm, vmem, hbm, hbm, hbm],
        out_specs=(vmem,) * 4,
        scratch_shapes=scratch,
        compiler_params=pltpu.CompilerParams(
            collective_id=0, has_side_effects=True, vmem_limit_bytes=56 * 2**20
        ),
        cost_estimate=pl.CostEstimate(flops=8 * 10**9, bytes_accessed=15 * 10**6, transcendentals=73728),
    )(tokens, out_grad, assignments.T, w_gate.swapaxes(1, 2), w_up.swapaxes(1, 2), w_down)
    in_grad, g_gate, g_up, g_down = pl.pallas_call(
        functools.partial(hand_over, 4),
        out_shape=(made(TOK, Q), made(1, FL, D), made(1, FL, D), made(1, FL, D)),
        in_specs=[vmem] * 4,
        out_specs=(hbm,) * 4,
        scratch_shapes=[S((4 * PARTS,))],
        compiler_params=pltpu.CompilerParams(vmem_limit_bytes=2 * 2**20),
                cost_estimate=pl.CostEstimate(flops=0, bytes_accessed=7 * 10**6, transcendentals=0),
    )(*[pltpu.with_memory_space_constraint(a, pltpu.VMEM) for a in made_here])
    return in_grad, g_gate.swapaxes(1, 2), g_up.swapaxes(1, 2), g_down


def solution(mesh):
    in_specs = (
        P("expert", None),
        P("expert", None),
        P("expert", None),
        P("expert", None, "dp"),
        P("expert", None, "dp"),
        P("expert", "dp", None),
    )
    out_specs = (
        P("expert", "dp"),
        P("expert", None, "dp"),
        P("expert", None, "dp"),
        P("expert", "dp", None),
    )
    return jax.shard_map(
        per_device, mesh=mesh, in_specs=in_specs, out_specs=out_specs, check_vma=False
    )
```

```python
import functools

import jax
import jax.numpy as jnp
from jax import lax
from jax.experimental import pallas as pl
from jax.experimental.pallas import tpu as pltpu
from jax.sharding import PartitionSpec as P

MESH = pl.DeviceIdType.MESH
BF, F32 = jnp.bfloat16, jnp.float32

D, FL, FP, CAP, TOK = 5120, 192, 256, 12, 256
Q, E8 = D // 4, D // 8
N_EXP = 32
PARTS = 4
CHUNKS = (
    ((1, 0), (3, 0), (0, 1), (0, 3)),
    ((1, 2), (3, 2), (2, 1), (2, 3)),
    ((1, 1), (3, 3), (1, 3), (3, 1)),
    ((2, 0), (0, 2), (0, 0), (2, 2)),
)
NC = len(CHUNKS)
G = 4
B = G * CAP
M = G * B
R = 2 * B
EX = ((0, R, 0), (R, R, 1), (2 * R, R, 2), (3 * R, B, 3), (3 * R + B, B, 4))
ALL = 2 * NC * B


def mm(a, b):
    return lax.dot_general(a, b, (((1,), (0,)), ((), ())), preferred_element_type=F32)


def mm_nt(a, b):
    return lax.dot_general(a, b, (((1,), (1,)), ((), ())), preferred_element_type=F32)


def mm_tn(a, b):
    return lax.dot_general(a, b, (((0,), (0,)), ((), ())), preferred_element_type=F32)


def iota(shape, dim):
    return lax.broadcasted_iota(jnp.int32, shape, dim)


def kernel(
    tok_hbm, grad_hbm, assign_ref, wg_hbm, wu_hbm, wd_hbm,
    o_in, o_gg, o_gu, o_gd,
    src, w_all, wt, codes, smat, perm, wide,
    pk_n, pk_c, rn, rc_relay, rc, rows, own, ex_send, ex_recv,
    zc_send, zc_recv, zn_send, zn_recv, ret_send, ret_recv, unp, dab_s, h_s, lhs,
    ld_sem, self_sem,
    pn_s, pn_r, pc_s, pc_r, zf_s, zf_r, sn_s, sn_r, sc_s, sc_r,
    ex_s, ex_r, zc_s, zc_r, zn_s, zn_r, rt_s, rt_r,
):
    e_idx, d_idx = lax.axis_index("expert"), lax.axis_index("dp")
    x, y, zl = e_idx // 8, (e_idx // 2) % 4, e_idx % 2
    zh, c = d_idx // 2, d_idx % 2

    def column(dx, dy):
        return ((x + dx) % 4) * 4 + (y + dy) % 4

    def plane(dx, dy):
        return (column(dx, dy) * 2 + zl, d_idx)

    def z_side(w):
        return ((x * 4 + y) * 2 + (1 - zl), 2 * w + c)

    z_far = (e_idx, 2 * (1 - zh) + c)
    sibling = (e_idx, 2 * zh + (1 - c))

    def remote(a, b, s, r, dev):
        return pltpu.make_async_remote_copy(
            src_ref=a, dst_ref=b, send_sem=s, recv_sem=r, device_id=dev, device_id_type=MESH
        )

    @pl.when(c == 0)
    def _():
        pltpu.make_async_copy(tok_hbm, src, ld_sem.at[0]).start()

    @pl.when(c == 1)
    def _():
        pltpu.make_async_copy(grad_hbm, src, ld_sem.at[0]).start()

    loads = [
        pltpu.make_async_copy(wg_hbm.at[0], w_all.at[pl.ds(0, FL)], ld_sem.at[1]),
        pltpu.make_async_copy(wu_hbm.at[0], w_all.at[pl.ds(FP, FL)], ld_sem.at[2]),
        pltpu.make_async_copy(wd_hbm.at[0], o_gd, ld_sem.at[3]),
    ]
    barrier = pltpu.get_barrier_semaphore()
    offsets = [o for ch in CHUNKS for o in ch]
    partners = [plane(*o) for o in offsets if o != (0, 0)]
    partners += [z_side(0), z_side(1), z_far, sibling]
    for dev in partners:
        pl.semaphore_signal(barrier, inc=1, device_id=dev, device_id_type=MESH)

    expert = iota((N_EXP, TOK), 0)
    member = jnp.zeros((N_EXP, TOK), F32)
    for k in range(assign_ref.shape[0]):
        member = member + jnp.where(assign_ref[k : k + 1, :] == expert, 1.0, 0.0)
    upto = jnp.where(iota((TOK, TOK), 0) <= iota((TOK, TOK), 1), 1.0, 0.0).astype(BF)
    codes[...] = member * mm(member.astype(BF), upto)
    row = iota((B, TOK), 0)
    grp, want = row // CAP, (row % CAP + 1).astype(F32)

    def choose(kind, k):
        z_of = 1 - zl if kind == 0 else zl
        code = jnp.zeros((B, TOK), F32)
        for i, o in enumerate(CHUNKS[k]):
            line = codes[pl.ds(column(*o) * 2 + z_of, 1), :]
            code = jnp.where(grp == i, jnp.broadcast_to(line, (B, TOK)), code)
        at = (kind * NC + k) * B
        smat[at : at + B, :] = jnp.where(code == want, 1.0, 0.0).astype(BF)

    choose(0, 0)
    r0, r1 = iota((M, M), 0), iota((M, M), 1)
    swapped = ((r0 // CAP) % 4) * B + (r0 // B) * CAP + r0 % CAP
    perm[...] = jnp.where(swapped == r1, 1.0, 0.0).astype(BF)

    pl.semaphore_wait(barrier, len(partners))
    pltpu.make_async_copy(tok_hbm, src, ld_sem.at[0]).wait()
    for load in loads:
        load.start()
    for a in range(2):
        w_all[a * FP + FL : (a + 1) * FP, :] = jnp.zeros((FP - FL, D), BF)

    def slot(k, i):
        return pl.ds(k * M + i * B, B)

    def chunk(k):
        return pl.ds(k * M, M)

    def send_n(k, i):
        return remote(pk_n.at[slot(k, i)], rn.at[c, slot(k, i)], pn_s.at[k * G + i], pn_r.at[k * G + i],
                      plane(*CHUNKS[k][i]))

    def send_c(k, i):
        return remote(pk_c.at[slot(k, i)], rc_relay.at[slot(k, i)], pc_s.at[k * G + i], pc_r.at[k * G + i],
                      plane(*CHUNKS[k][i]))

    def self_n(k, i):
        return pltpu.make_async_copy(pk_n.at[slot(k, i)], rn.at[c, slot(k, i)], self_sem.at[0])

    def self_c(k, i):
        return pltpu.make_async_copy(pk_c.at[slot(k, i)], rc_relay.at[slot(k, i)], self_sem.at[1])

    def pack_c(k):
        at = slice(k * B, (k + 1) * B)
        for j in range(4):
            cols = pl.ds(pl.multiple_of(zh * (D // 2) + j * E8, 128), E8)
            wide[at, j * E8 : (j + 1) * E8] = mm(smat[at, :], src[:, cols]).astype(BF)
        stack = jnp.concatenate([wide[at, j * E8 : (j + 1) * E8] for j in range(4)], axis=0)
        pk_c[chunk(k), :] = mm(perm[...], stack).astype(BF)

    def pack_n():
        for q in range(4):
            wide[:, q * Q : (q + 1) * Q] = mm(smat[M : 2 * M, :], src[:, q * Q : (q + 1) * Q]).astype(BF)
        for k in range(NC):
            stack = jnp.concatenate([wide[k * B : (k + 1) * B, q * Q : (q + 1) * Q] for q in range(4)], axis=0)
            pk_n[chunk(k), :] = mm(perm[...], stack).astype(BF)

    def go(k, far, near):
        for i, o in enumerate(CHUNKS[k]):
            (near if o == (0, 0) else far)(k, i).start()

    def sent(k, far):
        for i, o in enumerate(CHUNKS[k]):
            if o != (0, 0):
                far(k, i).wait_send()

    def come(k, far, near):
        for i, o in enumerate(CHUNKS[k]):
            if o == (0, 0):
                near(k, i).wait()
            else:
                far(k, i).wait_recv()

    def go_c(k):
        go(k, send_c, self_c)

    def go_n(k):
        go(k, send_n, self_n)

    def sent_c(k):
        sent(k, send_c)

    def sent_n(k):
        sent(k, send_n)

    def z_forward(k, w):
        return remote(rc_relay.at[chunk(k)], rc.at[c, zh, chunk(k)], zf_s.at[k * 2 + w], zf_r.at[k * 2 + zh],
                      z_side(w))

    def z_forward_in(k, w):
        return remote(rc_relay.at[chunk(k)], rc.at[c, w, chunk(k)], zf_s.at[k * 2 + w], zf_r.at[k * 2 + w],
                      z_side(w))

    def core_n(k, a):
        return remote(rn.at[a, chunk(k)], rn.at[a, chunk(k)], sn_s.at[k], sn_r.at[k], sibling)

    def core_c(k, a, w):
        return remote(rc.at[a, w, chunk(k)], rc.at[a, w, chunk(k)], sc_s.at[k * 2 + w], sc_r.at[k * 2 + w], sibling)

    def arrive_c(k):
        come(k, send_c, self_c)
        for w in range(2):
            z_forward(k, w).start()

    def arrive_n(k):
        come(k, send_n, self_n)
        core_n(k, c).start()

    def relay(k):
        for w in range(2):
            z_forward_in(k, w).wait_recv()
            core_c(k, c, w).start()

    def unpack(kind, pair, halves=(0, 1)):
        base = (kind * 2 + pair) * R
        for half in halves:
            k, at = pair * 2 + half, base + half * B
            if kind == 1:
                core_n(k, 1 - c).wait_recv()
                for a in range(2):
                    flat = mm(perm[...], rn[a, chunk(k), :]).astype(BF)
                    for q in range(4):
                        rows[a, at : at + B, q * Q : (q + 1) * Q] = flat[q * B : (q + 1) * B]
            else:
                for w in range(2):
                    core_c(k, 1 - c, w).wait_recv()
                for a in range(2):
                    for w in range(2):
                        flat = mm(perm[...], rc[a, w, chunk(k), :]).astype(BF)
                        for j in range(4):
                            col = w * (D // 2) + j * E8
                            rows[a, at : at + B, col : col + E8] = flat[j * B : (j + 1) * B]

    def hidden(base, m):

        def forward(q, acc):
            cols = pl.ds(pl.multiple_of(q * Q, 128), Q)
            xt = rows[0, pl.ds(base, m), cols]
            gt = rows[1, pl.ds(base, m), cols]
            return (
                acc[0] + mm(xt, wt[cols, 0 : 2 * FP]),
                acc[1] + mm(gt, wt[cols, 2 * FP : 3 * FP]),
            )

        ab, dh = lax.fori_loop(0, 4, forward, (jnp.zeros((m, 2 * FP), F32), jnp.zeros((m, FP), F32)))
        a_v, b_v = ab[:, :FP], ab[:, FP:]
        s_v = jax.nn.sigmoid(a_v)
        silu = a_v * s_v
        h_s[base : base + m, :] = (silu * b_v).astype(BF)
        dab_s[base : base + m, :FP] = (dh * b_v * s_v * (1.0 + a_v * (1.0 - s_v))).astype(BF)
        dab_s[base : base + m, FP:] = (dh * silu).astype(BF)

    def terms(base, m, part):
        group, lo = base // R, base % R
        at_rows = slice(lo, lo + m)

        def term(w, core):
            at = pl.ds(pl.multiple_of((2 * w + core) * Q, 128), Q)
            return mm(dab_s[base : base + m, :], w_all[0 : 2 * FP, at])

        for w in range(2):
            ex_send[group, w, at_rows] = term(w, 1 - c).astype(BF)
        core_ex(base, m, part).start()
        for w in range(2):
            own[group % 2, w, at_rows] = term(w, c)

    def core_ex(base, m, part):
        group, at = base // R, pl.ds(base % R, m)
        return remote(ex_send.at[group, :, at], ex_recv.at[group, :, at], ex_s.at[part], ex_r.at[part], sibling)

    def z_far_copy(k):
        return remote(zn_send.at[k], zn_recv.at[k], zn_s.at[k], zn_r.at[k], z_far)

    def go_far(k):
        z_far_copy(k).start()

    def z_side_copy(pair, w):
        return remote(zc_send.at[pair, w], zc_recv.at[pair, zh], zc_s.at[pair * 2 + w], zc_r.at[pair * 2 + zh],
                      z_side(w))

    def z_side_in(pair, w):
        return remote(zc_send.at[pair, w], zc_recv.at[pair, w], zc_s.at[pair * 2 + w], zc_r.at[pair * 2 + w],
                      z_side(w))

    def come_ex(part):
        core_ex(*EX[part]).wait_recv()

    def reduce_side(pair):
        group = pair
        core_ex(group * R, R, group).wait_recv()
        for w in range(2):
            zc_send[pair, w] = (own[pair, w] + ex_recv[group, w].astype(F32)).astype(BF)
            z_side_copy(pair, w).start()

    def reduce_far(k):
        pair, at = k // 2, pl.ds((k % 2) * B, B)
        far = own[pair, 1 - zh, at, :] + ex_recv[2 + pair, 1 - zh, at, :].astype(F32)
        zn_send[k] = far.astype(BF)

    def back(k, i):
        dx, dy = CHUNKS[k][i]
        return remote(ret_send.at[slot(k, i)], ret_recv.at[slot(k, i)], rt_s.at[k * G + i], rt_r.at[k * G + i],
                      plane(-dx, -dy))

    def self_back(k, i):
        return pltpu.make_async_copy(ret_send.at[slot(k, i)], ret_recv.at[slot(k, i)], self_sem.at[2])

    def give_back(k):
        pair, at = k // 2, pl.ds((k % 2) * B, B)
        if k % 2 == 0:
            for w in range(2):
                z_side_in(pair, w).wait_recv()
        z_far_copy(k).wait_recv()
        mine = own[pair, zh, at, :] + ex_recv[2 + pair, zh, at, :].astype(F32) + zn_recv[k].astype(F32)
        side = zc_recv[pair, 0, at, :].astype(F32) + zc_recv[pair, 1, at, :].astype(F32)
        mine, side = mine.astype(BF), side.astype(BF)
        stack = jnp.concatenate([mine[:, :E8], side[:, :E8], mine[:, E8:], side[:, E8:]], axis=0)
        ret_send[chunk(k), :] = mm(perm[...], stack).astype(BF)
        go(k, back, self_back)

    def collect(k):
        come(k, back, self_back)
        flat = mm(perm[...], ret_recv[chunk(k), :]).astype(BF)
        for hf in range(2):
            for kind in range(2):
                at, of = (kind * NC + k) * B, (hf * 2 + 1 - kind) * B
                unp[at : at + B, hf * E8 : (hf + 1) * E8] = flat[of : of + B]

    def turn_weights(part):
        loads[part].wait()
        tail = jnp.zeros((FP - FL, 512), BF)

        @pl.loop(0, 10)
        def _(t):
            cols = pl.ds(pl.multiple_of(t * 512, 128), 512)
            mine = o_gd[:, cols] if part == 2 else w_all[part * FP : part * FP + FL, cols]
            full = jnp.concatenate([mine, tail], axis=0)
            wt[cols, part * FP : (part + 1) * FP] = full.T

    def total():
        o_in[...] = mm(lhs[3 * FL :, :], unp[...]).astype(BF)

    def turn_rows():
        for a in range(2):
            lhs[a * FL : (a + 1) * FL, :] = dab_s[:, a * FP : (a + 1) * FP].astype(F32).T[0:FL].astype(BF)
        lhs[2 * FL : 3 * FL, :] = h_s[...].astype(F32).T[0:FL].astype(BF)
        lhs[3 * FL :, :] = smat[...].astype(F32).T.astype(BF)

    def wgrads(first, last):
        @pl.loop(first, last)
        def _(t):
            cols = pl.ds(pl.multiple_of(t * 512, 128), 512)
            both = mm(lhs[0 : 2 * FL, :], rows[0, :, cols])
            o_gg[:, cols] = both[0:FL].astype(BF)
            o_gu[:, cols] = both[FL : 2 * FL].astype(BF)
            o_gd[:, cols] = mm(lhs[2 * FL : 3 * FL, :], rows[1, :, cols]).astype(BF)

    pack_c(0)
    go_c(0)
    for k in range(1, NC):
        choose(0, k)
        pack_c(k)
    sent_c(0)
    go_c(1)
    for k in range(NC):
        choose(1, k)
    pack_n()
    arrive_c(0)
    sent_c(1)
    go_c(2)
    go_c(3)
    turn_weights(0)
    arrive_c(1)
    go_n(0)
    turn_weights(1)
    turn_weights(2)
    relay(0)
    sent_c(2)
    sent_c(3)
    go_n(1)
    relay(1)
    arrive_c(2)
    arrive_c(3)
    unpack(0, 0)
    hidden(*EX[0][:2])
    terms(*EX[0])
    reduce_side(0)
    arrive_n(0)
    arrive_n(1)
    go_n(2)
    relay(2)
    unpack(1, 0)
    hidden(*EX[2][:2])
    relay(3)
    terms(*EX[2])
    unpack(0, 1)
    come_ex(2)
    reduce_far(0)
    go_far(0)
    reduce_far(1)
    go_n(3)
    hidden(*EX[1][:2])
    go_far(1)
    arrive_n(2)
    terms(*EX[1])
    unpack(1, 1, (0,))
    reduce_side(1)
    hidden(*EX[3][:2])
    arrive_n(3)
    terms(*EX[3])
    give_back(0)
    unpack(1, 1, (1,))
    come_ex(3)
    reduce_far(2)
    go_far(2)
    give_back(1)
    hidden(*EX[4][:2])
    terms(*EX[4])
    turn_rows()
    come_ex(4)
    reduce_far(3)
    go_far(3)
    give_back(2)
    wgrads(0, 5)
    give_back(3)
    wgrads(5, 10)
    for k in range(NC):
        collect(k)
    total()
    def drain():
        for k in range(NC):
            sent_n(k)
        for k in range(NC):
            sent(k, back)
            for w in range(2):
                z_forward(k, w).wait_send()
                core_c(k, c, w).wait_send()
            core_n(k, c).wait_send()
        for pair in range(2):
            for w in range(2):
                z_side_copy(pair, w).wait_send()
        for k in range(NC):
            z_far_copy(k).wait_send()
        for ex in EX:
            core_ex(*ex).wait_send()

    drain()


def hand_over(n, *refs):
    src, dst, sem = refs[:n], refs[n : 2 * n], refs[2 * n]
    outs = []
    for i in range(n):
        to = dst[i] if i == 0 else dst[i].at[0]
        part = src[i].shape[0] // PARTS
        for p in range(PARTS):
            at = pl.ds(p * part, part)
            outs.append(pltpu.make_async_copy(src[i].at[at], to.at[at], sem.at[i * PARTS + p]))
    for cp in outs:
        cp.start()
    for cp in outs:
        cp.wait()


def per_device(tokens, out_grad, assignments, w_gate, w_up, w_down):
    hbm = pl.BlockSpec(memory_space=pl.ANY)
    vmem = pl.BlockSpec(memory_space=pltpu.VMEM)
    S = pltpu.SemaphoreType.DMA
    bf = lambda *shape: pltpu.VMEM(shape, BF)
    scratch = [
        bf(TOK, D), bf(2 * FP, D), bf(D, 3 * FP),
        pltpu.VMEM((N_EXP, TOK), F32), bf(ALL, TOK), bf(M, M), bf(M, D),
        bf(NC * M, Q), bf(NC * M, E8), bf(2, NC * M, Q), bf(NC * M, E8), bf(2, 2, NC * M, E8),
        bf(2, ALL, D), pltpu.VMEM((2, 2, R, Q), F32), bf(NC, 2, R, Q), bf(NC, 2, R, Q),
        bf(2, 2, R, Q), bf(2, 2, R, Q), bf(NC, B, Q), bf(NC, B, Q), bf(NC * M, E8), bf(NC * M, E8), bf(ALL, Q),
        bf(ALL, 2 * FP), bf(ALL, FP), bf(3 * FL + TOK, ALL),
        S((4,)), S((3,)),
        S((NC * G,)), S((NC * G,)), S((NC * G,)), S((NC * G,)),
        S((NC * 2,)), S((NC * 2,)), S((NC,)), S((NC,)), S((NC * 2,)), S((NC * 2,)),
        S((len(EX),)), S((len(EX),)), S((4,)), S((4,)), S((NC,)), S((NC,)), S((NC * G,)), S((NC * G,)),
    ]
    made = lambda *shape: jax.ShapeDtypeStruct(shape, BF)
    made_here = pl.pallas_call(
        kernel,
        out_shape=(bf(TOK, Q), bf(FL, D), bf(FL, D), bf(FL, D)),
        in_specs=[hbm, hbm, vmem, hbm, hbm, hbm],
        out_specs=(vmem,) * 4,
        scratch_shapes=scratch,
        compiler_params=pltpu.CompilerParams(
            collective_id=0, has_side_effects=True, vmem_limit_bytes=56 * 2**20
        ),
        cost_estimate=pl.CostEstimate(flops=8 * 10**9, bytes_accessed=15 * 10**6, transcendentals=73728),
    )(tokens, out_grad, assignments.T, w_gate.swapaxes(1, 2), w_up.swapaxes(1, 2), w_down)
    in_grad, g_gate, g_up, g_down = pl.pallas_call(
        functools.partial(hand_over, 4),
        out_shape=(made(TOK, Q), made(1, FL, D), made(1, FL, D), made(1, FL, D)),
        in_specs=[vmem] * 4,
        out_specs=(hbm,) * 4,
        scratch_shapes=[S((4 * PARTS,))],
        compiler_params=pltpu.CompilerParams(vmem_limit_bytes=2 * 2**20),
                cost_estimate=pl.CostEstimate(flops=0, bytes_accessed=7 * 10**6, transcendentals=0),
    )(*[pltpu.with_memory_space_constraint(a, pltpu.VMEM) for a in made_here])
    return in_grad, g_gate.swapaxes(1, 2), g_up.swapaxes(1, 2), g_down


def solution(mesh):
    in_specs = (
        P("expert", None),
        P("expert", None),
        P("expert", None),
        P("expert", None, "dp"),
        P("expert", None, "dp"),
        P("expert", "dp", None),
    )
    out_specs = (
        P("expert", "dp"),
        P("expert", None, "dp"),
        P("expert", None, "dp"),
        P("expert", "dp", None),
    )
    return jax.shard_map(
        per_device, mesh=mesh, in_specs=in_specs, out_specs=out_specs, check_vma=False
    )
```
